128 devices in a mesh: ctx: 32 (over x, z, core), tp: 4 (over y).
Axes of the slice: x: 4, y: 4, z: 4, core: 2. Of those that a mesh axis runs over, the one named last changes fastest.
Arguments:
- q_in: bfloat16 [8192, 8192], P('ctx', 'tp'), may hold values from -60 to 60
- k_in: bfloat16 [8192, 1024], P('ctx', 'tp'), may hold values from -6 to 6
- v_in: bfloat16 [8192, 1024], P('ctx', 'tp'), may hold values from -6 to 6
- doc_ids: int32 [8192], replicated, may hold values from 0 to 127, never falling along the last dimension, each value on 1 to 1024 neighbouring positions
- x_in: bfloat16 [8192, 16384], P('ctx', 'tp'), may hold values from -6 to 6
- b_in: bfloat16 [8192, 1024], P('ctx', 'tp'), may hold values from -6 to 6
- c_in: bfloat16 [8192, 1024], P('ctx', 'tp'), may hold values from -6 to 6
- z_gate: bfloat16 [8192, 16384], P('ctx', 'tp'), may hold values from -6 to 6
- dt_raw: bfloat16 [8192, 256], P('ctx', 'tp'), may hold values from -5 to 5
- conv_x: bfloat16 [4, 16384], P(None, 'tp'), may hold values from -3 to 3
- conv_b: bfloat16 [4, 1024], P(None, 'tp'), may hold values from -3 to 3
- conv_c: bfloat16 [4, 1024], P(None, 'tp'), may hold values from -3 to 3
- dt_bias: float32 [256], P('tp'), may hold values from -2 to 1
- rates: float32 [256], P('tp'), may hold values from 0.0002 to 0.05
- skip_d: float32 [256], P('tp'), may hold values from 0.5 to 1.5
- norm_gain: float32 [16384], P('tp'), may hold values from 0.5 to 1.5
Outputs:
- attn_out: bfloat16 [8192, 8192], P('ctx', 'tp')
- mamba_out: bfloat16 [8192, 16384], P('ctx', 'tp')
The draws below stay inside these ranges and needn't reach their ends.
Inputs may be any that keep to these rules, and one draw needn't show every extreme that they name: `doc_ids`: document ids never fall along the pack; a document covers 1 to 1024 tokens and one covers exactly 1024.
All inputs are finite; a program needn't handle non-finite values.
Results may differ from the reference program's by a relative error of at most 0.0065.
Values may be sent and summed in bfloat16 or wider, within the bound.
A program may use at most 192 MiB of HBM per device.

```python
import math
import jax
import jax.numpy as jnp
import numpy as np
from jax import lax

HEADS = 64
KV_HEADS = 8
HEAD_DIM = 128
SSM_HEADS = 256
SSM_HEAD_DIM = 64
STATE = 128
GROUPS = 8
CONV = 4
BLOCK = 128
DOC_SPAN = 4
TOK_DEV = 256
TOKENS = 8192
INNER = 16384
MOST = 1024
DOCS = 128


def keys_normal(key):
    return jnp.clip(jax.random.normal(key, (TOKENS, KV_HEADS * HEAD_DIM), jnp.float32), -6.0, 6.0)


def draw_k_in(key, part):
    base = keys_normal(key)
    return base.astype(jnp.bfloat16)


def draw_q_in(key, part):
    key = jax.random.fold_in(key, 7)
    result = jnp.clip(jax.random.normal(key, (TOKENS, HEADS * HEAD_DIM), jnp.float32), -6.0, 6.0)
    return result.astype(jnp.bfloat16)


def shard_levels(own_key, shape, cuts, smallest, largest):
    def one(dim, blocks):
        heights = jax.random.uniform(jax.random.fold_in(jax.random.fold_in(own_key, 6), dim), (blocks,), jnp.float32, smallest / len(cuts), largest / len(cuts))
        return jnp.repeat(jnp.exp(heights), shape[dim] // blocks).reshape((-1,) + (1,) * (len(shape) - dim - 1))

    loudness = one(*cuts[0])
    for cut in cuts[1:]:
        loudness = loudness * one(*cut)
    return loudness


def profile(count, total, most, slope):
    loads = [(1 << 20) // math.isqrt(standing ** slope) + 1 for standing in range(2, count + 1)]
    rest, counts = total - most - (count - 1), [1] * (count - 1)
    while rest > 0:
        candidates = [i for i in range(count - 1) if counts[i] < most]
        pool, remaining = sum([loads[i] for i in candidates]), rest
        for i in candidates:
            more = min(most - counts[i], max(1, remaining * loads[i] // pool), rest)
            counts[i] = counts[i] + more
            rest = rest - more
    return np.array([most] + counts)


def uneven(rng, number_of, total, most, lean):
    if number_of == 2:
        one = jax.random.randint(rng, (), max(1, total - most), min(most, total - 1) + 1)
        return jnp.stack([one, total - one])
    tallies = jnp.asarray(profile(number_of, total, most, lean), jnp.int32)
    pairs = (number_of - 1) // 2
    giver, taker = tallies[1:1 + 2 * pairs:2], tallies[2:2 + 2 * pairs:2]
    room = jnp.minimum(giver - 1, most - taker)
    shifted = jax.random.randint(jax.random.fold_in(rng, 1), (pairs,), 0, 1 << 20) % (room + 1)
    tallies = tallies.at[1:1 + 2 * pairs:2].set(giver - shifted).at[2:2 + 2 * pairs:2].set(taker + shifted)
    return tallies[jax.random.permutation(jax.random.fold_in(rng, 2), number_of)]


def gaussian(key, shape, deviation, most, cuts=(), kind=jnp.bfloat16):
    drawn = jax.random.normal(key, shape, jnp.float32) * deviation
    if len(cuts) > 0:
        drawn = shard_levels(key, shape, cuts, -0.22, 0.18) * drawn
    return jnp.clip(drawn, min=-most, max=most).astype(kind)


def setup_inputs(seed: int = 0) -> dict:
    splits = jax.random.split(jax.random.key(seed), 17)
    return {
        "q_in": draw_q_in(jax.random.fold_in(splits[16], 71), 0),
        "k_in": draw_k_in(jax.random.fold_in(splits[16], 71), 0),
        "v_in": gaussian(splits[2], (TOKENS, KV_HEADS * HEAD_DIM), 1.0, 6.0, ((0, 32), (1, 4))),
        "doc_ids": jnp.searchsorted(jnp.cumsum(uneven(splits[3], DOCS, TOKENS, MOST, 2)), jnp.arange(TOKENS), side="right").astype(jnp.int32),
        "x_in": gaussian(splits[4], (TOKENS, INNER), 1.0, 6.0, ((0, 32), (1, 4))),
        "b_in": gaussian(splits[5], (TOKENS, GROUPS * STATE), 1.0, 6.0, ((0, 32), (1, 4))),
        "c_in": gaussian(splits[6], (TOKENS, GROUPS * STATE), 1.0, 6.0, ((0, 32), (1, 4))),
        "z_gate": gaussian(splits[7], (TOKENS, INNER), 1.0, 6.0, ((0, 32), (1, 4))),
        "dt_raw": gaussian(splits[8], (TOKENS, SSM_HEADS), 1.0, 5.0, ((0, 32), (1, 4))),
        "conv_x": gaussian(splits[9], (CONV, INNER), CONV ** -0.5, 3.0, ((1, 4),)),
        "conv_b": gaussian(splits[10], (CONV, GROUPS * STATE), CONV ** -0.5, 3.0, ((1, 4),)),
        "conv_c": gaussian(splits[11], (CONV, GROUPS * STATE), CONV ** -0.5, 3.0, ((1, 4),)),
        "dt_bias": jnp.clip(-2.0 + 3.0 * jax.random.uniform(splits[12], (SSM_HEADS,), jnp.float32) ** shard_levels(splits[12], (SSM_HEADS,), ((0, 4),), -0.2, 0.2), -2.0, 1.0),
        "rates": jnp.clip(jnp.exp(math.log(0.05) - 5.521461 * jax.random.uniform(splits[13], (SSM_HEADS,), jnp.float32) ** shard_levels(splits[13], (SSM_HEADS,), ((0, 4),), -0.2, 0.2)), 0.0002, 0.05),
        "skip_d": jnp.clip(0.5 + 1.0 * jax.random.uniform(splits[14], (SSM_HEADS,), jnp.float32) ** shard_levels(splits[14], (SSM_HEADS,), ((0, 4),), -0.2, 0.2), 0.5, 1.5),
        "norm_gain": jnp.clip(1.0 + 0.1 * jax.random.normal(splits[15], (INNER,), jnp.float32), 0.5, 1.5),
    }


NEGATIVE = -1e+30
EPSILON = 1e-05

def conv_rows(window, weights, window_ids):
    taps = weights.shape[0]
    count = window.shape[0] - taps + 1
    own_ids = window_ids[taps - 1:]
    total = jnp.zeros((count, window.shape[1]), jnp.float32)
    for offset in range(taps):
        keep = (window_ids[offset:offset + count] == own_ids).astype(jnp.float32)
        total = total + weights[offset].astype(jnp.float32)[None, :] * window[offset:offset + count].astype(jnp.float32) * keep[:, None]
    return jax.nn.silu(total).astype(jnp.bfloat16)

def ssd_block(inputs_x, inputs_b, inputs_c, steps_dt, log_decay, block_ids, prev_id, state_in):
    block_len = inputs_x.shape[0]
    num_heads = inputs_x.shape[1]
    per_group = num_heads // inputs_b.shape[1]
    cumul = jnp.cumsum(log_decay, axis=0)
    places = jnp.arange(block_len, dtype=jnp.int32)
    allowed = (block_ids[:, None] == block_ids[None, :]) & (places[:, None] >= places[None, :])
    affinity = jnp.einsum('tgn,sgn->gts', inputs_c.astype(jnp.float32), inputs_b.astype(jnp.float32), precision=lax.Precision.HIGHEST)
    affinity = jnp.repeat(affinity, per_group, axis=0)
    cumul_heads = cumul.T
    gaps = jnp.where(allowed[None], cumul_heads[:, :, None] - cumul_heads[:, None, :], 0.0)
    decay = jnp.where(allowed[None], jnp.exp(gaps), 0.0)
    mixing = (affinity * decay * steps_dt.T[:, None, :]).astype(jnp.bfloat16)
    inside = jnp.einsum('hts,shp->thp', mixing.astype(jnp.float32), inputs_x.astype(jnp.float32), precision=lax.Precision.HIGHEST)
    carried_on = (block_ids == prev_id).astype(jnp.float32)[:, None] * jnp.exp(cumul)
    c_heads = jnp.repeat(inputs_c, per_group, axis=1).astype(jnp.float32)
    from_state = jnp.einsum('thn,hpn->thp', c_heads, state_in, precision=lax.Precision.HIGHEST)
    outputs = inside + carried_on[:, :, None] * from_state
    last_id = block_ids[block_len - 1]
    end_weight = jnp.exp(cumul[block_len - 1][None, :] - cumul) * steps_dt * (block_ids == last_id).astype(jnp.float32)[:, None]
    b_heads = jnp.repeat(inputs_b, per_group, axis=1).astype(jnp.float32)
    weighted_b = (b_heads * end_weight[:, :, None]).astype(jnp.bfloat16)
    fresh = jnp.einsum('shn,shp->hpn', weighted_b.astype(jnp.float32), inputs_x.astype(jnp.float32), precision=lax.Precision.HIGHEST)
    keep_state = jnp.where(last_id == prev_id, jnp.exp(cumul[block_len - 1]), 0.0)
    return (outputs, fresh + keep_state[:, None, None] * state_in)

def reference(q_in, k_in, v_in, doc_ids, x_in, b_in, c_in, z_gate, dt_raw, conv_x, conv_b, conv_c, dt_bias, rates, skip_d, norm_gain):
    group_size = HEADS // KV_HEADS
    reach = DOC_SPAN * TOK_DEV
    span_len = reach + TOK_DEV
    scale = HEAD_DIM ** (-0.5)

    def attend_block(index):
        first = index * TOK_DEV
        key_first = jnp.maximum(first - reach, 0)
        queries = lax.dynamic_slice_in_dim(q_in, first, TOK_DEV, 0).reshape(TOK_DEV, KV_HEADS, group_size, HEAD_DIM)
        keys = lax.dynamic_slice_in_dim(k_in, key_first, span_len, 0).reshape(span_len, KV_HEADS, HEAD_DIM)
        values = lax.dynamic_slice_in_dim(v_in, key_first, span_len, 0).reshape(span_len, KV_HEADS, HEAD_DIM)
        query_ids = lax.dynamic_slice_in_dim(doc_ids, first, TOK_DEV)
        key_ids = lax.dynamic_slice_in_dim(doc_ids, key_first, span_len)
        query_pos = first + jnp.arange(TOK_DEV, dtype=jnp.int32)
        key_pos = key_first + jnp.arange(span_len, dtype=jnp.int32)
        allowed = (query_ids[:, None] == key_ids[None, :]) & (query_pos[:, None] >= key_pos[None, :])

        def one_head(head):
            query_head = lax.dynamic_index_in_dim(queries, head, 1, False).astype(jnp.float32)
            key_head = lax.dynamic_index_in_dim(keys, head, 1, False).astype(jnp.float32)
            value_head = lax.dynamic_index_in_dim(values, head, 1, False).astype(jnp.float32)
            scores = jnp.einsum('tgd,sd->gts', query_head, key_head, precision=lax.Precision.HIGHEST) * scale
            masked = jnp.where(allowed[None], scores, NEGATIVE)
            top = lax.optimization_barrier(jnp.max(masked, axis=-1))
            probs = jnp.where(allowed[None], jnp.exp(masked - top[..., None]), 0.0)
            total = lax.optimization_barrier(jnp.sum(probs, axis=-1))
            weights = probs.astype(jnp.bfloat16).astype(jnp.float32)
            summed = jnp.einsum('gts,sd->tgd', weights, value_head, precision=lax.Precision.HIGHEST)
            return summed / jnp.transpose(total)[:, :, None]
        per_head = lax.map(one_head, jnp.arange(KV_HEADS, dtype=jnp.int32))
        return jnp.transpose(per_head, (1, 0, 2, 3)).reshape(TOK_DEV, HEADS * HEAD_DIM).astype(jnp.bfloat16)
    attn_out = lax.map(attend_block, jnp.arange(TOKENS // TOK_DEV, dtype=jnp.int32)).reshape(TOKENS, HEADS * HEAD_DIM)

    def ssm_step(carry, index):
        state, prev_id = carry
        first = index * BLOCK
        prior_first = jnp.maximum(first - (CONV - 1), 0)
        prior_pos = first - (CONV - 1) + jnp.arange(CONV - 1, dtype=jnp.int32)
        prior_ids = jnp.where(prior_pos >= 0, lax.dynamic_slice_in_dim(doc_ids, prior_first, CONV - 1), -1)
        block_ids = lax.dynamic_slice_in_dim(doc_ids, first, BLOCK)
        window_ids = jnp.concatenate([prior_ids, block_ids])

        def window(source):
            return jnp.concatenate([lax.dynamic_slice_in_dim(source, prior_first, CONV - 1, 0), lax.dynamic_slice_in_dim(source, first, BLOCK, 0)])
        x_conv = conv_rows(window(x_in), conv_x, window_ids)
        b_conv = conv_rows(window(b_in), conv_b, window_ids)
        c_conv = conv_rows(window(c_in), conv_c, window_ids)
        steps_dt = jax.nn.softplus(lax.dynamic_slice_in_dim(dt_raw, first, BLOCK, 0).astype(jnp.float32) + dt_bias[None, :])
        log_decay = -steps_dt * rates[None, :]
        outputs, new_state = ssd_block(x_conv.reshape(BLOCK, SSM_HEADS, SSM_HEAD_DIM), b_conv.reshape(BLOCK, GROUPS, STATE), c_conv.reshape(BLOCK, GROUPS, STATE), steps_dt, log_decay, block_ids, prev_id, state)
        full = outputs + skip_d[None, :, None] * x_conv.reshape(BLOCK, SSM_HEADS, SSM_HEAD_DIM).astype(jnp.float32)
        gates = lax.dynamic_slice_in_dim(z_gate, first, BLOCK, 0).astype(jnp.float32)
        gated = full.reshape(BLOCK, INNER) * jax.nn.silu(gates)
        squares = lax.optimization_barrier(jnp.sum(gated * gated, axis=1))
        result = (gated * lax.rsqrt(squares / INNER + EPSILON)[:, None] * norm_gain[None, :]).astype(jnp.bfloat16)
        return ((new_state, block_ids[BLOCK - 1]), result)
    start = (jnp.zeros((SSM_HEADS, SSM_HEAD_DIM, STATE), jnp.float32), jnp.array(-1, jnp.int32))
    _final, blocks_out = lax.scan(ssm_step, start, jnp.arange(TOKENS // BLOCK, dtype=jnp.int32))
    mamba_out = blocks_out.reshape(TOKENS, INNER)
    return (attn_out, mamba_out)
```

```python
import functools

import jax
import jax.numpy as jnp
from jax import lax
from jax.experimental import pallas as pl
from jax.experimental.pallas import tpu as pltpu
from jax.sharding import PartitionSpec as P

HEAD_DIM = 128
STATE = 128
INNER = 16384
EPSILON = 1e-05
FAR = 1e30
LOG2E = 1.4426950408889634

TOK = 256
WIDE = 512
MESH = pl.DeviceIdType.MESH
F32 = jnp.float32
BF16 = jnp.bfloat16

RIM_X, RIM_B, RIM_C, K1, V1, K2, V2, KX, VX, K1S, V1S, E_SIB, T_SIB, E_C1, E_C2, T_C, IN_SIB, SQ = range(18)
COPIES = SQ + 3
L_X, L_Z, L_Q, L_K, L_V, L_B, L_C, L_AO, L_MO = range(9)


def dot(a, b):
    return lax.dot_general(a, b, (((1,), (0,)), ((), ())), preferred_element_type=F32)


def dot_nt(a, b):
    return lax.dot_general(a, b, (((1,), (1,)), ((), ())), preferred_element_type=F32)


def silu(a):
    half = 0.5 * a
    return half + half * jnp.tanh(half)


def repeat_lanes(a, times):
    return jnp.concatenate([a] * times, axis=1)


def split2(a):
    high = a.astype(BF16).astype(F32)
    return jnp.concatenate([high, a - high], axis=1).astype(BF16)


def kernel(
    n_ctx,
    n_tp,
    q_hbm,
    k_hbm,
    v_hbm,
    ids,
    x_hbm,
    b_hbm,
    c_hbm,
    z_hbm,
    dt_raw,
    conv_x,
    conv_b,
    conv_c,
    dt_bias,
    rates,
    skip_d,
    gain,
    ao_hbm,
    mo_hbm,
    xv,
    zv,
    qv,
    kbuf,
    vbuf,
    bv,
    cv,
    rim_x,
    rim_b,
    rim_c,
    g1,
    gate,
    e_own,
    e_sib,
    e_chip,
    e_n1,
    e_n2,
    in_own,
    in_sib,
    t_own,
    t_sib,
    t_chip,
    t_n1,
    sq_own,
    sq_in,
    expand,
    shift,
    mix,
    bt,
    cj,
    far_own,
    hot,
    tri_bias,
    ao,
    mo,
    sumsq,
    send,
    recv,
    local,
):
    p = lax.axis_index("ctx")
    t = lax.axis_index("tp")
    core = lax.rem(p, 2)
    sib = p + 1 - 2 * core
    channels = x_hbm.shape[1]
    groups = channels // 2048
    half_width = channels // 2

    def at(offset):
        return lax.rem(p + offset + n_ctx, n_ctx)

    def remote(src, dst, slot, to, tp=None):
        return pltpu.make_async_remote_copy(
            src_ref=src,
            dst_ref=dst,
            send_sem=send.at[slot],
            recv_sem=recv.at[slot],
            device_id=(to, t if tp is None else tp),
            device_id_type=MESH,
        )

    loads = {
        L_B: pltpu.make_async_copy(b_hbm, bv, local.at[L_B]),
        L_C: pltpu.make_async_copy(c_hbm, cv, local.at[L_C]),
        L_X: pltpu.make_async_copy(x_hbm, xv, local.at[L_X]),
        L_Z: pltpu.make_async_copy(z_hbm, zv, local.at[L_Z]),
        L_K: pltpu.make_async_copy(k_hbm, kbuf.at[0], local.at[L_K]),
        L_V: pltpu.make_async_copy(v_hbm, vbuf.at[0], local.at[L_V]),
        L_Q: pltpu.make_async_copy(q_hbm, qv, local.at[L_Q]),
    }

    barrier = pltpu.get_barrier_semaphore()
    for source in (sib, at(-1), at(-2), at(-4)):
        pl.semaphore_signal(barrier, inc=1, device_id=(source, t), device_id_type=MESH)
    for step in range(1, n_tp):
        pl.semaphore_signal(
            barrier, inc=1, device_id=(p, lax.rem(t + n_tp - step, n_tp)), device_id_type=MESH
        )
    for slot in (L_B, L_C, L_X, L_Z, L_K, L_V, L_Q):
        loads[slot].start()
    pl.semaphore_wait(barrier, 4 + n_tp - 1)

    last_rows = pl.ds(TOK - 16, 16)
    rims = [
        remote(b_hbm.at[last_rows], rim_b, RIM_B, at(1)),
        remote(c_hbm.at[last_rows], rim_c, RIM_C, at(1)),
        remote(x_hbm.at[last_rows], rim_x, RIM_X, at(1)),
    ]
    for copy in rims:
        copy.start()
    near = [
        remote(k_hbm, kbuf.at[1], K1, at(2)),
        remote(v_hbm, vbuf.at[1], V1, at(2)),
    ]
    far = [
        remote(k_hbm, kbuf.at[3], K2, at(4)),
        remote(v_hbm, vbuf.at[3], V2, at(4)),
    ]
    for copy in near + far:
        copy.start()
    own_to_sib = [
        remote(k_hbm, kbuf.at[4], KX, sib),
        remote(v_hbm, vbuf.at[4], VX, sib),
    ]

    @pl.when(core == 0)
    def _():
        for copy in own_to_sib:
            copy.start()

    def id_row(row):
        return ids[pl.ds(row, 1), :].astype(F32)

    def id_column(row):
        return jnp.broadcast_to(id_row(row), (128, 128)).T

    def id_columns(device):
        return jnp.concatenate([id_column(2 * device), id_column(2 * device + 1)], axis=0)

    own_cols = id_columns(p)
    own_row = jnp.concatenate([id_row(2 * p), id_row(2 * p + 1)], axis=1)
    last_id = own_row[:, TOK - 1 : TOK]
    before_row = lax.rem(2 * p - 1 + 2 * n_ctx, 2 * n_ctx)
    first_device = p == 0
    before_cols = jnp.where(first_device, -1.0, id_column(before_row))
    before_id = jnp.where(first_device, -1.0, id_row(before_row))[:, 127:128]
    lanes = lax.broadcasted_iota(jnp.int32, (TOK, 128), 1).astype(F32)
    far_own[...] = jnp.where(own_cols == lanes, 0.0, -FAR).astype(BF16)
    block_devices = (p, p - 2, p - 1 - 2 * core, p - 4, p - 3 + 2 * core)
    for slot, device in enumerate(block_devices):
        columns = id_columns(lax.rem(device + n_ctx, n_ctx)) if slot else own_cols
        hot[slot] = jnp.where(columns == lanes, 1.0, 0.0).astype(BF16)
    row_at = lax.broadcasted_iota(jnp.int32, (TOK, TOK), 0)
    col_at = lax.broadcasted_iota(jnp.int32, (TOK, TOK), 1)
    same = repeat_lanes(own_cols, 2) == own_row
    causal = col_at <= row_at
    allowed = same & causal
    tri_bias[...] = jnp.where(causal, 0.0, -FAR)
    for back in range(1, 4):
        shift[pl.ds((back - 1) * TOK, TOK), :] = jnp.where(
            same & (row_at - col_at == back), 1.0, 0.0
        ).astype(BF16)
    tops = lax.broadcasted_iota(jnp.int32, (8, 128), 0)
    rim_keep = [
        jnp.where(
            (tops < back) & (own_cols[:8] == pltpu.roll(before_cols[120:], back, 0)), 1.0, 0.0
        )
        for back in range(1, 4)
    ]

    raw = dt_raw[...].astype(F32) + dt_bias[...]
    steps = jnp.maximum(raw, 0.0) + jnp.log(1.0 + jnp.exp(-jnp.abs(raw)))
    log_decay = -steps * rates[...]
    upto = jnp.where(causal, 1.0, 0.0).astype(BF16)
    part = log_decay.astype(BF16)
    rest = log_decay - part.astype(F32)
    part2 = rest.astype(BF16)
    part3 = (rest - part2.astype(F32)).astype(BF16)
    cum = dot(upto, part) + (dot(upto, part2) + dot(upto, part3))
    middle = cum[TOK // 2 - 1 : TOK // 2]
    end = cum[TOK - 1 : TOK]
    expand[pl.ds(0, TOK), :] = split2(jnp.exp(middle - cum) * steps)
    expand[pl.ds(TOK, TOK), :] = split2(jnp.exp(cum - middle))
    continues = before_id == last_id
    through = jnp.where(continues, jnp.exp(end), 0.0)
    wide_through = jnp.concatenate([through, through], axis=1)
    t_own[...] = jnp.broadcast_to(wide_through, (8, 128))
    rows = lax.broadcasted_iota(jnp.int32, (16, 64), 0)
    vectors = jnp.where(rows == 0, jnp.exp(end - middle), jnp.where(rows == 1, skip_d[...], 0.0))
    expand[pl.ds(2 * TOK, 16), :] = split2(vectors)
    middle_factor = jnp.exp(middle)

    def spread_matrix(tile):
        head = lax.broadcasted_iota(jnp.int32, (128, WIDE), 0) & 63
        place = (lax.broadcasted_iota(jnp.int32, (128, WIDE), 1) >> 6) + tile * (WIDE // 64)
        return jnp.where(head == place, 1.0, 0.0).astype(BF16)

    def conv(source, rim, weights, width):
        moved = dot(shift[...], source)
        taps = weights.astype(F32)
        total = taps[3:4] * source.astype(F32)
        edge = jnp.zeros((8, width), F32)
        rim8 = rim.astype(F32)[8:16]
        for back in range(1, 4):
            tap = taps[3 - back : 4 - back]
            total = total + tap * moved[(back - 1) * TOK : back * TOK]
            keep = repeat_lanes(rim_keep[back - 1], width // 128)
            edge = edge + tap * (keep * pltpu.roll(rim8, back, 0))
        total = jnp.concatenate([total[:8] + edge, total[8:]], axis=0)
        return silu(total).astype(BF16)

    for slot in (L_B, L_C):
        loads[slot].wait()
    for copy in rims:
        copy.wait()
    b_conv = conv(bv[...], rim_b[...], conv_b[...], bv.shape[1])
    c_conv = conv(cv[...], rim_c[...], conv_c[...], cv.shape[1])
    for group in range(groups):
        b_group = b_conv[:, group * STATE : (group + 1) * STATE]
        c_group = c_conv[:, group * STATE : (group + 1) * STATE]
        mix[group] = jnp.where(allowed, dot_nt(c_group, b_group), 0.0).astype(BF16)
        ending = jnp.where(own_cols == last_id, b_group.astype(F32), 0.0)
        bt[group] = ending.T.astype(BF16)
        cj[group] = jnp.where(own_cols == before_id, c_group.astype(F32), 0.0).astype(BF16)

    loads[L_X].wait()
    loads[L_Z].wait()
    tiles_per_group = 2048 // WIDE

    def ssd_tile(tile, carry):
        group = tile // tiles_per_group
        here = pl.ds(pl.multiple_of(tile * WIDE, WIDE), WIDE)
        x_conv = conv(xv[:, here], rim_x[:, here], conv_x[:, here], WIDE)
        factors = dot(expand[...], spread_matrix(tile))
        x_wide = x_conv.astype(F32)
        x_scaled = (x_wide * factors[:TOK]).astype(BF16)
        inside = dot(mix[group], x_scaled)
        e_own[:, here] = (dot(bt[group], x_scaled) * factors[2 * TOK : 2 * TOK + 1]).astype(BF16)
        open_gate = silu(zv[:, here].astype(F32))
        leaving = factors[TOK : 2 * TOK]
        full = leaving * inside + factors[2 * TOK + 1 : 2 * TOK + 2] * x_wide
        g1[:, here] = full * open_gate
        gate[:, here] = leaving * open_gate
        return carry

    lax.fori_loop(0, channels // WIDE, ssd_tile, 0)

    to_sib = [remote(e_own, e_sib, E_SIB, sib), remote(t_own, t_sib, T_SIB, sib)]
    for copy in to_sib:
        copy.start()
    for copy in near:
        copy.wait()
    sib_near = [
        remote(kbuf.at[1], kbuf.at[2], K1S, sib),
        remote(vbuf.at[1], vbuf.at[2], V1S, sib),
    ]
    for copy in sib_near:
        copy.start()
    for copy in to_sib:
        copy.wait()

    t_chip[...] = t_own[...] * t_sib[...]
    is_low = core == 0
    u_own = split2(jnp.where(is_low, t_sib[...], 1.0)[:, :64])
    u_sib = split2(jnp.where(is_low, 1.0, t_own[...])[:, :64])
    u_both = jnp.concatenate([u_own, u_sib], axis=0)
    half_tiles = half_width // WIDE

    def chip_tile(tile, carry):
        whole = core * half_tiles + tile
        here = pl.ds(pl.multiple_of(tile * WIDE, WIDE), WIDE)
        there = pl.ds(pl.multiple_of(whole * WIDE, WIDE), WIDE)
        factors = dot(u_both, spread_matrix(whole))
        e_chip[:, here] = (
            factors[0:1] * e_own[:, there].astype(F32) + factors[8:9] * e_sib[:, there].astype(F32)
        ).astype(BF16)
        return carry

    lax.fori_loop(0, half_tiles, chip_tile, 0)
    chip_sends = [
        remote(t_chip, t_n1, T_C, at(2)),
        remote(e_chip, e_n1, E_C1, at(2)),
        remote(e_chip, e_n2, E_C2, at(4)),
    ]
    for copy in chip_sends:
        copy.start()

    for copy in far:
        copy.wait()
    far_to_sib = [
        remote(kbuf.at[3], kbuf.at[4], KX, sib),
        remote(vbuf.at[3], vbuf.at[4], VX, sib),
    ]

    @pl.when(core == 1)
    def _():
        for copy in far_to_sib:
            copy.start()
            copy.wait_send()

    @pl.when(core == 0)
    def _():
        for copy in own_to_sib:
            copy.wait_send()

    for copy in far_to_sib:
        copy.wait_recv()
    for copy in sib_near:
        copy.wait()
    for slot in (L_K, L_V, L_Q):
        loads[slot].wait()

    factor = HEAD_DIM**-0.5 * LOG2E
    query_heads = q_hbm.shape[1] // HEAD_DIM
    per_kv = query_heads // (k_hbm.shape[1] // HEAD_DIM)

    def attend(head, carry):
        here = pl.ds(pl.multiple_of(head * HEAD_DIM, HEAD_DIM), HEAD_DIM)
        kv = pl.ds(pl.multiple_of((head // per_kv) * HEAD_DIM, HEAD_DIM), HEAD_DIM)
        query = jnp.concatenate([qv[:, here], far_own[...]], axis=1)
        scores = []
        for slot in range(5):
            key = jnp.concatenate([kbuf[slot, :, kv], hot[slot]], axis=1)
            scores.append(dot_nt(query, key))
        scores[0] = scores[0] + tri_bias[...]
        top = functools.reduce(jnp.maximum, scores)
        top = jnp.max(top, axis=1, keepdims=True) * factor
        ones = jnp.ones((TOK, HEAD_DIM), BF16)
        summed = jnp.zeros((TOK, 2 * HEAD_DIM), F32)
        for slot in range(5):
            weights = jnp.exp2(scores[slot] * factor - top).astype(BF16)
            value = jnp.concatenate([vbuf[slot, :, kv], ones], axis=1)
            summed = summed + dot(weights, value)
        ao[:, here] = (summed[:, :HEAD_DIM] / summed[:, HEAD_DIM:]).astype(BF16)
        return carry

    lax.fori_loop(0, query_heads, attend, 0)
    ao_out = pltpu.make_async_copy(ao, ao_hbm, local.at[L_AO])
    ao_out.start()

    for copy in chip_sends:
        copy.wait()
    u_chip = split2(t_n1[...][:, :64])

    def in_tile(tile, carry):
        here = pl.ds(pl.multiple_of(tile * WIDE, WIDE), WIDE)
        factors = dot(u_chip, spread_matrix(core * half_tiles + tile))
        in_own[:, here] = (
            e_n1[:, here].astype(F32) + factors[0:1] * e_n2[:, here].astype(F32)
        ).astype(BF16)
        return carry

    lax.fori_loop(0, half_tiles, in_tile, 0)
    swap = remote(in_own, in_sib, IN_SIB, sib)
    swap.start()

    w_sib = split2(jnp.where(is_low, 0.0, jnp.broadcast_to(middle_factor, (8, 64))))
    w_in = split2(jnp.where(is_low, 1.0, t_sib[...])[:, :64] * middle_factor)
    w_both = jnp.concatenate([w_sib, w_in], axis=0)
    sumsq[...] = jnp.zeros_like(sumsq)

    def join_tiles(incoming, first):
        def join_tile(tile, carry):
            whole = first + tile
            group = whole // tiles_per_group
            here = pl.ds(pl.multiple_of(tile * WIDE, WIDE), WIDE)
            there = pl.ds(pl.multiple_of(whole * WIDE, WIDE), WIDE)
            factors = dot(w_both, spread_matrix(whole))
            state = factors[0:1] * e_sib[:, there].astype(F32) + factors[8:9] * incoming[
                :, here
            ].astype(F32)
            gated = g1[:, there] + gate[:, there] * dot(cj[group], state.astype(BF16))
            g1[:, there] = gated
            squares = gated * gated
            total = sumsq[...]
            for lane in range(WIDE // 128):
                total = total + squares[:, lane * 128 : (lane + 1) * 128]
            sumsq[...] = total
            return carry

        lax.fori_loop(0, half_tiles, join_tile, 0)

    join_tiles(in_own, core * half_tiles)
    swap.wait()
    join_tiles(in_sib, (1 - core) * half_tiles)

    own_sums = jnp.concatenate(
        [
            jnp.sum(sumsq[pl.ds(0, 128), :].T, axis=0, keepdims=True),
            jnp.sum(sumsq[pl.ds(128, 128), :].T, axis=0, keepdims=True),
        ],
        axis=1,
    )
    sq_own[...] = jnp.broadcast_to(own_sums, (8, TOK))
    sq_sends = [
        remote(sq_own, sq_in.at[step - 1], SQ + step - 1, p, lax.rem(t + step, n_tp))
        for step in range(1, n_tp)
    ]
    for copy in sq_sends:
        copy.start()
    for copy in sq_sends:
        copy.wait()
    total = sq_own[...]
    for step in range(1, n_tp):
        total = total + sq_in[step - 1]
    scale = lax.rsqrt(total[0:1] / INNER + EPSILON)
    scale_cols = jnp.concatenate(
        [
            jnp.broadcast_to(scale[:, :128], (128, 128)).T,
            jnp.broadcast_to(scale[:, 128:], (128, 128)).T,
        ],
        axis=0,
    )
    scale_wide = repeat_lanes(scale_cols, WIDE // 128)

    def norm_tile(tile, carry):
        here = pl.ds(pl.multiple_of(tile * WIDE, WIDE), WIDE)
        mo[:, here] = (g1[:, here] * scale_wide * gain[:, here]).astype(BF16)
        return carry

    lax.fori_loop(0, channels // WIDE, norm_tile, 0)
    mo_out = pltpu.make_async_copy(mo, mo_hbm, local.at[L_MO])
    mo_out.start()
    ao_out.wait()
    mo_out.wait()


def per_device(q, k, v, ids, x, b, c, z, dt_raw, conv_x, conv_b, conv_c, dt_bias, rates, skip_d, gain):
    n_ctx, n_tp = lax.axis_size("ctx"), lax.axis_size("tp")
    channels = x.shape[1]
    half = channels // 2
    groups = b.shape[1] // STATE
    hbm = pl.BlockSpec(memory_space=pl.ANY)
    vmem = pl.BlockSpec(memory_space=pltpu.VMEM)
    specs = [hbm, hbm, hbm, vmem, hbm, hbm, hbm, hbm] + [vmem] * 8
    scratch = [
        pltpu.VMEM(x.shape, BF16),
        pltpu.VMEM(z.shape, BF16),
        pltpu.VMEM(q.shape, BF16),
        pltpu.VMEM((5,) + k.shape, BF16),
        pltpu.VMEM((5,) + v.shape, BF16),
        pltpu.VMEM(b.shape, BF16),
        pltpu.VMEM(c.shape, BF16),
        pltpu.VMEM((16, channels), BF16),
        pltpu.VMEM((16, b.shape[1]), BF16),
        pltpu.VMEM((16, c.shape[1]), BF16),
        pltpu.VMEM(x.shape, F32),
        pltpu.VMEM(x.shape, F32),
        pltpu.VMEM((STATE, channels), BF16),
        pltpu.VMEM((STATE, channels), BF16),
        pltpu.VMEM((STATE, half), BF16),
        pltpu.VMEM((STATE, half), BF16),
        pltpu.VMEM((STATE, half), BF16),
        pltpu.VMEM((STATE, half), BF16),
        pltpu.VMEM((STATE, half), BF16),
        pltpu.VMEM((8, 128), F32),
        pltpu.VMEM((8, 128), F32),
        pltpu.VMEM((8, 128), F32),
        pltpu.VMEM((8, 128), F32),
        pltpu.VMEM((8, TOK), F32),
        pltpu.VMEM((n_tp - 1, 8, TOK), F32),
        pltpu.VMEM((2 * TOK + 16, 128), BF16),
        pltpu.VMEM((3 * TOK, TOK), BF16),
        pltpu.VMEM((groups, TOK, TOK), BF16),
        pltpu.VMEM((groups, STATE, TOK), BF16),
        pltpu.VMEM((groups, TOK, STATE), BF16),
        pltpu.VMEM((TOK, 128), BF16),
        pltpu.VMEM((5, TOK, 128), BF16),
        pltpu.VMEM((TOK, TOK), F32),
        pltpu.VMEM(q.shape, BF16),
        pltpu.VMEM(x.shape, BF16),
        pltpu.VMEM((TOK, 128), F32),
        pltpu.SemaphoreType.DMA((COPIES,)),
        pltpu.SemaphoreType.DMA((COPIES,)),
        pltpu.SemaphoreType.DMA((9,)),
    ]
    return pl.pallas_call(
        functools.partial(kernel, n_ctx, n_tp),
        out_shape=(
            jax.ShapeDtypeStruct(q.shape, BF16),
            jax.ShapeDtypeStruct(x.shape, BF16),
        ),
        in_specs=specs,
        out_specs=(hbm, hbm),
        scratch_shapes=scratch,
        compiler_params=pltpu.CompilerParams(
            collective_id=1, has_side_effects=True, vmem_limit_bytes=56 * 2**20
        ),
        name="packed_mix",
    )(
        q,
        k,
        v,
        ids.reshape(-1, 128),
        x,
        b,
        c,
        z,
        dt_raw,
        conv_x,
        conv_b,
        conv_c,
        dt_bias[None],
        rates[None],
        skip_d[None],
        gain[None],
    )


def solution(mesh):
    both = P("ctx", "tp")
    placed = (both, both, both, P(), both, both, both, both, both)
    placed += (P(None, "tp"),) * 3 + (P("tp"),) * 4
    return jax.shard_map(
        per_device, mesh=mesh, in_specs=placed, out_specs=(both, both), check_vma=False
    )
```

```python
import functools

import jax
import jax.numpy as jnp
from jax import lax
from jax.experimental import pallas as pl
from jax.experimental.pallas import tpu as pltpu
from jax.sharding import PartitionSpec as P

HEAD_DIM = 128
STATE = 128
INNER = 16384
EPSILON = 1e-05
FAR = 1e30
LOG2E = 1.4426950408889634

TOK = 256
WIDE = 512
Z_CHIPS = 4
MESH = pl.DeviceIdType.MESH
F32 = jnp.float32
BF16 = jnp.bfloat16

CHUNKS = 4
RIM_X, RIM_B, RIM_C, K1, V1, KZ, K2, V2, KX, VX, K1S, V1S, E_A, E_B, T_SIB, T_C = range(16)
E1 = 16
EZ = E1 + CHUNKS
E2 = EZ + CHUNKS
IN = E2 + CHUNKS
SQ = IN + CHUNKS
COPIES = SQ + 3
L_X, L_Z, L_Q, L_K, L_V, L_B, L_C, L_AO, L_MO = range(9)


def dot(a, b):
    return lax.dot_general(a, b, (((1,), (0,)), ((), ())), preferred_element_type=F32)


def dot_nt(a, b):
    return lax.dot_general(a, b, (((1,), (1,)), ((), ())), preferred_element_type=F32)


def silu(a):
    half = 0.5 * a
    return half + half * jnp.tanh(half)


def repeat_lanes(a, times):
    return jnp.concatenate([a] * times, axis=1)


def split2(a):
    high = a.astype(BF16).astype(F32)
    lane = lax.broadcasted_iota(jnp.int32, a.shape, 1)
    return jnp.where(lane < 64, high, a - high).astype(BF16)


def kernel(
    n_ctx,
    n_tp,
    q_hbm,
    k_hbm,
    v_hbm,
    ids,
    x_hbm,
    b_hbm,
    c_hbm,
    z_hbm,
    dt_raw,
    conv_x,
    conv_b,
    conv_c,
    dt_bias,
    rates,
    skip_d,
    gain,
    ao_hbm,
    mo_hbm,
    xv,
    zv,
    qv,
    kbuf,
    vbuf,
    k_pass,
    bv,
    cv,
    rim_x,
    rim_b,
    rim_c,
    xs,
    g1,
    gate,
    e_own,
    e_sib,
    e_chip,
    e_n1,
    e_n2,
    e_pass,
    in_own,
    in_sib,
    t_own,
    t_sib,
    t_chip,
    t_n1,
    sq_own,
    sq_in,
    expand,
    expand_in,
    spread_in,
    shift,
    mix,
    bt,
    cj,
    far_own,
    hot,
    tri_bias,
    ao,
    mo,
    sumsq,
    send,
    recv,
    local,
):
    p = lax.axis_index("ctx")
    t = lax.axis_index("tp")
    core = lax.rem(p, 2)
    sib = p + 1 - 2 * core
    channels = x_hbm.shape[1]
    groups = bv.shape[1] // STATE
    tiles = channels // WIDE
    per_group = tiles // groups
    chip = p // 2
    x_at, z_at = chip // Z_CHIPS, lax.rem(chip, Z_CHIPS)
    x_chips = n_ctx // (2 * Z_CHIPS)

    def chip_device(x, z):
        return (lax.rem(x, x_chips) * Z_CHIPS + lax.rem(z, Z_CHIPS)) * 2 + core

    wraps = ((z_at == 1) | (z_at == 2)).astype(jnp.int32)
    pass_to = chip_device(x_at + wraps, z_at + Z_CHIPS - 1)
    lower = chip_device(x_at, z_at + Z_CHIPS - 1)
    upper = chip_device(x_at, z_at + 1)
    upper_wraps = ((z_at == 0) | (z_at == 1)).astype(jnp.int32)
    pass_from = chip_device(x_at + x_chips - upper_wraps, z_at + 1)

    def at(offset):
        return lax.rem(p + offset + n_ctx, n_ctx)

    def remote(src, dst, slot, to, tp=None):
        return pltpu.make_async_remote_copy(
            src_ref=src,
            dst_ref=dst,
            send_sem=send.at[slot],
            recv_sem=recv.at[slot],
            device_id=(to, t if tp is None else tp),
            device_id_type=MESH,
        )

    loads = {
        L_B: pltpu.make_async_copy(b_hbm, bv, local.at[L_B]),
        L_C: pltpu.make_async_copy(c_hbm, cv, local.at[L_C]),
        L_X: pltpu.make_async_copy(x_hbm, xv, local.at[L_X]),
        L_Z: pltpu.make_async_copy(z_hbm, zv, local.at[L_Z]),
        L_K: pltpu.make_async_copy(k_hbm, kbuf.at[0], local.at[L_K]),
        L_V: pltpu.make_async_copy(v_hbm, vbuf.at[0], local.at[L_V]),
        L_Q: pltpu.make_async_copy(q_hbm, qv, local.at[L_Q]),
    }

    barrier = pltpu.get_barrier_semaphore()
    for source in (sib, at(-1), at(-2), upper, pass_from):
        pl.semaphore_signal(barrier, inc=1, device_id=(source, t), device_id_type=MESH)
    for step in range(1, n_tp):
        pl.semaphore_signal(
            barrier, inc=1, device_id=(p, lax.rem(t + n_tp - step, n_tp)), device_id_type=MESH
        )
    for slot in (L_B, L_C, L_X, L_Z, L_K, L_V, L_Q):
        loads[slot].start()
    pl.semaphore_wait(barrier, 5 + n_tp - 1)

    last_rows = pl.ds(TOK - 16, 16)
    rims = [
        remote(b_hbm.at[last_rows], rim_b, RIM_B, at(1)),
        remote(c_hbm.at[last_rows], rim_c, RIM_C, at(1)),
        remote(x_hbm.at[last_rows], rim_x, RIM_X, at(1)),
    ]
    for copy in rims:
        copy.start()
    near = [
        remote(v_hbm, vbuf.at[1], V1, at(2)),
        remote(k_hbm, kbuf.at[1], K1, at(2)),
    ]
    k_down = remote(k_hbm, k_pass, KZ, lower)
    far = [
        remote(vbuf.at[1], vbuf.at[3], V2, at(2)),
        remote(k_pass, kbuf.at[3], K2, pass_to),
    ]
    for copy in near:
        copy.start()
    k_down.start()
    own_to_sib = [
        remote(k_hbm, kbuf.at[4], KX, sib),
        remote(v_hbm, vbuf.at[4], VX, sib),
    ]

    @pl.when(core == 0)
    def _():
        for copy in own_to_sib:
            copy.start()

    def id_row(row):
        return ids[pl.ds(row, 1), :].astype(F32)

    def id_column(row):
        return jnp.broadcast_to(id_row(row), (128, 128)).T

    def id_columns(device):
        return jnp.concatenate([id_column(2 * device), id_column(2 * device + 1)], axis=0)

    own_cols = id_columns(p)
    own_row = jnp.concatenate([id_row(2 * p), id_row(2 * p + 1)], axis=1)
    last_id = own_row[:, TOK - 1 : TOK]
    before_row = lax.rem(2 * p - 1 + 2 * n_ctx, 2 * n_ctx)
    first_device = p == 0
    before_cols = jnp.where(first_device, -1.0, id_column(before_row))
    before_id = jnp.where(first_device, -1.0, id_row(before_row))[:, 127:128]
    lanes = lax.broadcasted_iota(jnp.int32, (TOK, 128), 1).astype(F32)
    far_own[...] = jnp.where(own_cols == lanes, 0.0, -FAR).astype(BF16)
    block_devices = (p, p - 2, p - 1 - 2 * core, p - 4, p - 3 + 2 * core)
    for slot, device in enumerate(block_devices):
        columns = id_columns(lax.rem(device + n_ctx, n_ctx)) if slot else own_cols
        hot[slot] = jnp.where(columns == lanes, 1.0, 0.0).astype(BF16)
    row_at = lax.broadcasted_iota(jnp.int32, (TOK, TOK), 0)
    col_at = lax.broadcasted_iota(jnp.int32, (TOK, TOK), 1)
    same = repeat_lanes(own_cols, 2) == own_row
    causal = col_at <= row_at
    allowed = same & causal
    tri_bias[...] = jnp.where(causal, 0.0, -FAR)
    for back in range(1, 4):
        shift[pl.ds((back - 1) * TOK, TOK), :] = jnp.where(
            same & (row_at - col_at == back), 1.0, 0.0
        ).astype(BF16)
    tops = lax.broadcasted_iota(jnp.int32, (8, 128), 0)
    rim_keep = [
        jnp.where(
            (tops < back) & (own_cols[:8] == pltpu.roll(before_cols[120:], back, 0)), 1.0, 0.0
        )
        for back in range(1, 4)
    ]

    raw = dt_raw[...].astype(F32)
    raw = jnp.concatenate([raw, raw], axis=0).T + repeat_lanes(dt_bias[...], 2)
    steps = jnp.maximum(raw, 0.0) + jnp.log(1.0 + jnp.exp(-jnp.abs(raw)))
    log_decay = -steps * repeat_lanes(rates[...], 2)
    upto = jnp.where(causal, 1.0, 0.0).astype(BF16)
    part = log_decay.astype(BF16)
    rest = log_decay - part.astype(F32)
    part2 = rest.astype(BF16)
    part3 = (rest - part2.astype(F32)).astype(BF16)
    cum = dot(upto, part) + (dot(upto, part2) + dot(upto, part3))
    middle = cum[TOK // 2 - 1 : TOK // 2]
    end = cum[TOK - 1 : TOK]
    expand[pl.ds(0, TOK), :] = split2(jnp.exp(middle - cum) * steps)
    expand[pl.ds(TOK, TOK), :] = split2(jnp.exp(cum - middle))
    continues = before_id == last_id
    through = jnp.where(continues, jnp.exp(end), 0.0)
    t_own[...] = jnp.broadcast_to(through, (8, 128))
    t_send = remote(t_own, t_sib, T_SIB, sib)
    t_send.start()

    def spread_matrix(tile):
        head = lax.broadcasted_iota(jnp.int32, (128, WIDE), 0) & 63
        place = (lax.broadcasted_iota(jnp.int32, (128, WIDE), 1) >> 6) + tile * (WIDE // 64)
        return jnp.where(head == place, 1.0, 0.0).astype(BF16)

    def conv(source, rim, weights, width):
        moved = dot(shift[...], source)
        taps = weights.astype(F32)
        total = taps[3:4] * source.astype(F32)
        edge = jnp.zeros((8, width), F32)
        rim8 = rim.astype(F32)[8:16]
        for back in range(1, 4):
            tap = taps[3 - back : 4 - back]
            total = total + tap * moved[(back - 1) * TOK : back * TOK]
            keep = repeat_lanes(rim_keep[back - 1], width // 128)
            edge = edge + tap * (keep * pltpu.roll(rim8, back, 0))
        total = jnp.concatenate([total[:8] + edge, total[8:]], axis=0)
        return silu(total).astype(BF16)

    for slot in (L_B, L_C):
        loads[slot].wait()
    for copy in rims[:2]:
        copy.wait()
    b_conv = conv(bv[...], rim_b[...], conv_b[...], bv.shape[1])
    c_conv = conv(cv[...], rim_c[...], conv_c[...], cv.shape[1])
    for group in range(groups):
        b_group = b_conv[:, group * STATE : (group + 1) * STATE]
        c_group = c_conv[:, group * STATE : (group + 1) * STATE]
        mix[group] = jnp.where(allowed, dot_nt(c_group, b_group), 0.0).astype(BF16)
        ending = jnp.where(own_cols == last_id, b_group.astype(F32), 0.0)
        bt[group] = ending.T.astype(BF16)
        cj[group] = jnp.where(own_cols == before_id, c_group.astype(F32), 0.0).astype(BF16)

    t_send.wait()
    t_chip[...] = t_own[...] * t_sib[...]
    t_next = remote(t_chip, t_n1, T_C, at(2))
    t_next.start()
    is_low = core == 0
    rows = lax.broadcasted_iota(jnp.int32, (16, 128), 0)
    vectors = jnp.where(rows == 0, jnp.exp(end - middle), 0.0)
    vectors = jnp.where(rows == 1, repeat_lanes(skip_d[...], 2), vectors)
    vectors = jnp.where(rows == 2, jnp.where(is_low, t_sib[0:1], 1.0), vectors)
    vectors = jnp.where(rows == 3, jnp.where(is_low, 1.0, t_own[0:1]), vectors)
    expand[pl.ds(2 * TOK, 16), :] = split2(vectors)

    loads[L_X].wait()
    rims[2].wait()

    def end_state(tile):
        here = pl.ds(pl.multiple_of(tile * WIDE, WIDE), WIDE)
        x_conv = conv(xv[:, here], rim_x[:, here], conv_x[:, here], WIDE)
        xv[:, here] = x_conv
        spread = spread_matrix(tile)
        factors = dot(expand[pl.ds(0, TOK), :], spread)
        vectors = dot(expand[pl.ds(2 * TOK, 16), :], spread)
        x_scaled = (x_conv.astype(F32) * factors).astype(BF16)
        xs[:, here] = x_scaled
        state = dot(bt[tile // per_group], x_scaled) * vectors[0:1]
        e_own[tile] = state.astype(BF16)
        return state, vectors

    mine, others = core * CHUNKS, (1 - core) * CHUNKS

    def other_half(chunk, carry):
        end_state(others + chunk)
        return carry

    lax.fori_loop(0, CHUNKS, other_half, 0, unroll=2)
    half_a = remote(e_own.at[pl.ds(others, CHUNKS)], e_sib.at[pl.ds(others, CHUNKS)], E_A, sib)
    half_a.start()

    for copy in near + [k_down]:
        copy.wait()
    sib_near = [
        remote(kbuf.at[1], kbuf.at[2], K1S, sib),
        remote(vbuf.at[1], vbuf.at[2], V1S, sib),
    ]
    for copy in far + sib_near:
        copy.start()

    nears = [remote(e_chip.at[i], e_n1.at[i], E1 + i, at(2)) for i in range(CHUNKS)]
    downs = [remote(e_chip.at[i], e_pass.at[i], EZ + i, lower) for i in range(1, CHUNKS)]
    for chunk in range(CHUNKS):
        state, vectors = end_state(mine + chunk)
        if chunk == 0:
            half_a.wait()
        e_chip[chunk] = (
            vectors[2:3] * state + vectors[3:4] * e_sib[mine + chunk].astype(F32)
        ).astype(BF16)
        nears[chunk].start()
        if chunk:
            downs[chunk - 1].start()
    half_b = remote(e_own.at[pl.ds(mine, CHUNKS)], e_sib.at[pl.ds(mine, CHUNKS)], E_B, sib)
    half_b.start()

    loads[L_Z].wait()

    def gate_tile(tile, carry):
        here = pl.ds(pl.multiple_of(tile * WIDE, WIDE), WIDE)
        spread = spread_matrix(tile)
        leaving = dot(expand[pl.ds(TOK, TOK), :], spread)
        vectors = dot(expand[pl.ds(2 * TOK, 16), :], spread)
        open_gate = silu(zv[:, here].astype(F32))
        full = leaving * dot(mix[tile // per_group], xs[:, here]) + vectors[1:2] * xv[
            :, here
        ].astype(F32)
        g1[:, here] = full * open_gate
        gate[:, here] = leaving * open_gate
        return carry

    lax.fori_loop(0, tiles, gate_tile, 0, unroll=2)

    for copy in far:
        copy.wait()
    far_to_sib = [
        remote(kbuf.at[3], kbuf.at[4], KX, sib),
        remote(vbuf.at[3], vbuf.at[4], VX, sib),
    ]

    @pl.when(core == 1)
    def _():
        for copy in far_to_sib:
            copy.start()
        for copy in far_to_sib:
            copy.wait_send()

    @pl.when(core == 0)
    def _():
        for copy in own_to_sib:
            copy.wait_send()

    for copy in far_to_sib:
        copy.wait_recv()
    for copy in sib_near:
        copy.wait()
    for slot in (L_K, L_V, L_Q):
        loads[slot].wait()

    factor = HEAD_DIM**-0.5 * LOG2E
    query_heads = q_hbm.shape[1] // HEAD_DIM
    per_kv = query_heads // (k_hbm.shape[1] // HEAD_DIM)

    def attend(head, carry):
        here = pl.ds(pl.multiple_of(head * HEAD_DIM, HEAD_DIM), HEAD_DIM)
        kv = pl.ds(pl.multiple_of((head // per_kv) * HEAD_DIM, HEAD_DIM), HEAD_DIM)
        query = jnp.concatenate([qv[:, here], far_own[...]], axis=1)
        scores = []
        for slot in range(5):
            key = jnp.concatenate([kbuf[slot, :, kv], hot[slot]], axis=1)
            scores.append(dot_nt(query, key))
        scores[0] = scores[0] + tri_bias[...]
        top = functools.reduce(jnp.maximum, scores)
        top = jnp.max(top, axis=1, keepdims=True) * factor
        ones = jnp.ones((TOK, HEAD_DIM), BF16)
        summed = jnp.zeros((TOK, 2 * HEAD_DIM), F32)
        for slot in range(5):
            weights = jnp.exp2(scores[slot] * factor - top).astype(BF16)
            value = jnp.concatenate([vbuf[slot, :, kv], ones], axis=1)
            summed = summed + dot(weights, value)
        ao[:, here] = (summed[:, :HEAD_DIM] / summed[:, HEAD_DIM:]).astype(BF16)
        return carry

    per_part = query_heads // CHUNKS

    def attend_part(part, carry):
        lax.fori_loop(part * per_part, (part + 1) * per_part, attend, 0, unroll=True)

        @pl.when(part < CHUNKS - 1)
        def _():
            remote(e_chip.at[part], e_pass.at[part + 1], EZ + part + 1, lower).wait_recv()
            remote(e_pass.at[part + 1], e_n2.at[part + 1], E2 + part + 1, pass_to).start()

        @pl.when(part == 0)
        def _():
            nears[0].wait_recv()
            remote(e_n1.at[0], e_n2.at[0], E2, at(2)).start()

        return carry

    lax.fori_loop(0, CHUNKS, attend_part, 0)
    ao_out = pltpu.make_async_copy(ao, ao_hbm, local.at[L_AO])
    ao_out.start()

    t_next.wait()
    half_b.wait()
    vectors = jnp.where(rows == 0, jnp.where(is_low, 0.0, jnp.exp(middle)), 0.0)
    vectors = jnp.where(rows == 1, jnp.where(is_low, 1.0, t_sib[0:1]) * jnp.exp(middle), vectors)
    vectors = jnp.where(rows == 2, t_n1[0:1], vectors)
    expand_in[...] = split2(vectors)

    def spread_tile(tile, carry):
        spread_in[tile] = dot(expand_in[...], spread_matrix(tile))
        return carry

    lax.fori_loop(0, tiles, spread_tile, 0)
    sumsq[...] = jnp.zeros_like(sumsq)

    def join_tile(tile, incoming):
        here = pl.ds(pl.multiple_of(tile * WIDE, WIDE), WIDE)
        vectors = spread_in[tile]
        state = vectors[0:1] * e_sib[tile].astype(F32) + vectors[1:2] * incoming
        gated = g1[:, here] + gate[:, here] * dot(cj[tile // per_group], state.astype(BF16))
        g1[:, here] = gated
        squares = gated * gated
        total = sumsq[...]
        for lane in range(WIDE // 128):
            total = total + squares[:, lane * 128 : (lane + 1) * 128]
        sumsq[...] = total

    swaps = [remote(in_own.at[i], in_sib.at[i], IN + i, sib) for i in range(CHUNKS)]
    for chunk in range(CHUNKS):
        tile = mine + chunk
        if chunk == 0:
            passed = remote(e_n1.at[0], e_n2.at[0], E2, at(2))
            nears[0].wait_send()
        else:
            passed = remote(e_pass.at[chunk], e_n2.at[chunk], E2 + chunk, pass_to)
            nears[chunk].wait()
            downs[chunk - 1].wait_send()
        passed.wait()
        arriving = e_n1[chunk].astype(F32) + spread_in[tile][2:3] * e_n2[chunk].astype(F32)
        in_own[chunk] = arriving.astype(BF16)
        swaps[chunk].start()
        join_tile(tile, arriving)
    for chunk in range(CHUNKS):
        swaps[chunk].wait()
        join_tile(others + chunk, in_sib[chunk].astype(F32))

    own_sums = jnp.concatenate(
        [
            jnp.sum(sumsq[pl.ds(0, 128), :].T, axis=0, keepdims=True),
            jnp.sum(sumsq[pl.ds(128, 128), :].T, axis=0, keepdims=True),
        ],
        axis=1,
    )
    sq_own[...] = jnp.broadcast_to(own_sums, (8, TOK))
    sq_sends = [
        remote(sq_own, sq_in.at[step - 1], SQ + step - 1, p, lax.rem(t + step, n_tp))
        for step in range(1, n_tp)
    ]
    for copy in sq_sends:
        copy.start()
    for copy in sq_sends:
        copy.wait()
    total = sq_own[...]
    for step in range(1, n_tp):
        total = total + sq_in[step - 1]
    scale = lax.rsqrt(total[0:1] / INNER + EPSILON)
    scale_cols = jnp.concatenate(
        [
            jnp.broadcast_to(scale[:, :128], (128, 128)).T,
            jnp.broadcast_to(scale[:, 128:], (128, 128)).T,
        ],
        axis=0,
    )
    scale_wide = repeat_lanes(scale_cols, WIDE // 128)

    outs = []
    for tile in range(tiles):
        here = slice(tile * WIDE, (tile + 1) * WIDE)
        mo[:, here] = (g1[:, here] * scale_wide * gain[:, here]).astype(BF16)
        out = pltpu.make_async_copy(
            mo.at[:, pl.ds(tile * WIDE, WIDE)],
            mo_hbm.at[:, pl.ds(tile * WIDE, WIDE)],
            local.at[L_MO + tile],
        )
        out.start()
        outs.append(out)
    ao_out.wait()
    for out in outs:
        out.wait()


def per_device(q, k, v, ids, x, b, c, z, dt_raw, conv_x, conv_b, conv_c, dt_bias, rates, skip_d, gain):
    n_ctx, n_tp = lax.axis_size("ctx"), lax.axis_size("tp")
    channels = x.shape[1]
    tiles = channels // WIDE
    groups = b.shape[1] // STATE
    hbm = pl.BlockSpec(memory_space=pl.ANY)
    vmem = pl.BlockSpec(memory_space=pltpu.VMEM)
    specs = [hbm, hbm, hbm, vmem, hbm, hbm, hbm, hbm] + [vmem] * 8
    scratch = [
        pltpu.VMEM(x.shape, BF16),
        pltpu.VMEM(z.shape, BF16),
        pltpu.VMEM(q.shape, BF16),
        pltpu.VMEM((5,) + k.shape, BF16),
        pltpu.VMEM((5,) + v.shape, BF16),
        pltpu.VMEM(k.shape, BF16),
        pltpu.VMEM(b.shape, BF16),
        pltpu.VMEM(c.shape, BF16),
        pltpu.VMEM((16, channels), BF16),
        pltpu.VMEM((16, b.shape[1]), BF16),
        pltpu.VMEM((16, c.shape[1]), BF16),
        pltpu.VMEM(x.shape, BF16),
        pltpu.VMEM(x.shape, F32),
        pltpu.VMEM(x.shape, F32),
        pltpu.VMEM((tiles, STATE, WIDE), BF16),
        pltpu.VMEM((tiles, STATE, WIDE), BF16),
        pltpu.VMEM((CHUNKS, STATE, WIDE), BF16),
        pltpu.VMEM((CHUNKS, STATE, WIDE), BF16),
        pltpu.VMEM((CHUNKS, STATE, WIDE), BF16),
        pltpu.VMEM((CHUNKS, STATE, WIDE), BF16),
        pltpu.VMEM((CHUNKS, STATE, WIDE), BF16),
        pltpu.VMEM((CHUNKS, STATE, WIDE), BF16),
        pltpu.VMEM((8, 128), F32),
        pltpu.VMEM((8, 128), F32),
        pltpu.VMEM((8, 128), F32),
        pltpu.VMEM((8, 128), F32),
        pltpu.VMEM((8, TOK), F32),
        pltpu.VMEM((n_tp - 1, 8, TOK), F32),
        pltpu.VMEM((2 * TOK + 16, 128), BF16),
        pltpu.VMEM((16, 128), BF16),
        pltpu.VMEM((tiles, 16, WIDE), F32),
        pltpu.VMEM((3 * TOK, TOK), BF16),
        pltpu.VMEM((groups, TOK, TOK), BF16),
        pltpu.VMEM((groups, STATE, TOK), BF16),
        pltpu.VMEM((groups, TOK, STATE), BF16),
        pltpu.VMEM((TOK, 128), BF16),
        pltpu.VMEM((5, TOK, 128), BF16),
        pltpu.VMEM((TOK, TOK), F32),
        pltpu.VMEM(q.shape, BF16),
        pltpu.VMEM(x.shape, BF16),
        pltpu.VMEM((TOK, 128), F32),
        pltpu.SemaphoreType.DMA((COPIES,)),
        pltpu.SemaphoreType.DMA((COPIES,)),
        pltpu.SemaphoreType.DMA((L_MO + tiles,)),
    ]
    return pl.pallas_call(
        functools.partial(kernel, n_ctx, n_tp),
        out_shape=(
            jax.ShapeDtypeStruct(q.shape, BF16),
            jax.ShapeDtypeStruct(x.shape, BF16),
        ),
        in_specs=specs,
        out_specs=(hbm, hbm),
        scratch_shapes=scratch,
        compiler_params=pltpu.CompilerParams(
            collective_id=1, has_side_effects=True, vmem_limit_bytes=56 * 2**20
        ),
        name="packed_mix",
    )(
        q,
        k,
        v,
        ids.reshape(-1, 128),
        x,
        b,
        c,
        z,
        dt_raw.T,
        conv_x,
        conv_b,
        conv_c,
        dt_bias[None],
        rates[None],
        skip_d[None],
        gain[None],
    )


def solution(mesh):
    both = P("ctx", "tp")
    placed = (both, both, both, P(), both, both, both, both, both)
    placed += (P(None, "tp"),) * 3 + (P("tp"),) * 4
    return jax.shard_map(
        per_device, mesh=mesh, in_specs=placed, out_specs=(both, both), check_vma=False
    )
```

```python
import functools

import jax
import jax.numpy as jnp
from jax import lax
from jax.experimental import pallas as pl
from jax.experimental.pallas import tpu as pltpu
from jax.sharding import PartitionSpec as P

HEAD_DIM = 128
STATE = 128
INNER = 16384
EPSILON = 1e-05
FAR = 1e30
LOG2E = 1.4426950408889634

TOK = 256
WIDE = 512
Z_CHIPS = 4
MESH = pl.DeviceIdType.MESH
F32 = jnp.float32
BF16 = jnp.bfloat16

CHUNKS = 4
PIECE = 256
PIECES = CHUNKS * WIDE // PIECE
FORWARD = (0, 2, 4)
RIM_X, RIM_B, RIM_C, K1, V1, KZ, K2, V2, KX, VX, K1S, V1S, E_B, T_SIB, T_C = range(15)
E_A = 15
E1 = E_A + CHUNKS
EZ = E1 + PIECES
E2 = EZ + PIECES
IN = E2 + PIECES
SQ = IN + CHUNKS
COPIES = SQ + 3
L_X, L_Z, L_Q, L_K, L_V, L_B, L_C, L_AO, L_MO = range(9)


def dot(a, b):
    return lax.dot_general(a, b, (((1,), (0,)), ((), ())), preferred_element_type=F32)


def dot_nt(a, b):
    return lax.dot_general(a, b, (((1,), (1,)), ((), ())), preferred_element_type=F32)


def silu(a):
    half = 0.5 * a
    return half + half * jnp.tanh(half)


def repeat_lanes(a, times):
    return jnp.concatenate([a] * times, axis=1)


def split2(a):
    high = a.astype(BF16).astype(F32)
    lane = lax.broadcasted_iota(jnp.int32, a.shape, 1)
    return jnp.where(lane < 64, high, a - high).astype(BF16)


def kernel(
    n_ctx,
    n_tp,
    q_hbm,
    k_hbm,
    v_hbm,
    ids,
    x_hbm,
    b_hbm,
    c_hbm,
    z_hbm,
    dt_raw,
    conv_x,
    conv_b,
    conv_c,
    dt_bias,
    rates,
    skip_d,
    gain,
    ao_hbm,
    mo_hbm,
    xv,
    zv,
    qv,
    kbuf,
    vbuf,
    k_pass,
    bv,
    cv,
    rim_x,
    rim_b,
    rim_c,
    xs,
    g1,
    gate,
    e_own,
    e_sib,
    e_chip,
    e_n1,
    e_n2,
    e_pass,
    in_own,
    in_sib,
    t_own,
    t_sib,
    t_chip,
    t_n1,
    sq_own,
    sq_in,
    expand,
    expand_in,
    spread_in,
    shift,
    mix,
    bt,
    cj,
    far_own,
    hot,
    tri_bias,
    ao,
    mo,
    sumsq,
    send,
    recv,
    local,
):
    p = lax.axis_index("ctx")
    t = lax.axis_index("tp")
    core = lax.rem(p, 2)
    sib = p + 1 - 2 * core
    channels = x_hbm.shape[1]
    groups = bv.shape[1] // STATE
    tiles = channels // WIDE
    per_group = tiles // groups
    chip = p // 2
    x_at, z_at = chip // Z_CHIPS, lax.rem(chip, Z_CHIPS)
    x_chips = n_ctx // (2 * Z_CHIPS)

    def chip_device(x, z):
        return (lax.rem(x, x_chips) * Z_CHIPS + lax.rem(z, Z_CHIPS)) * 2 + core

    wraps = ((z_at == 1) | (z_at == 2)).astype(jnp.int32)
    pass_to = chip_device(x_at + wraps, z_at + Z_CHIPS - 1)
    lower = chip_device(x_at, z_at + Z_CHIPS - 1)
    upper = chip_device(x_at, z_at + 1)
    upper_wraps = ((z_at == 0) | (z_at == 1)).astype(jnp.int32)
    pass_from = chip_device(x_at + x_chips - upper_wraps, z_at + 1)

    def at(offset):
        return lax.rem(p + offset + n_ctx, n_ctx)

    def remote(src, dst, slot, to, tp=None):
        return pltpu.make_async_remote_copy(
            src_ref=src,
            dst_ref=dst,
            send_sem=send.at[slot],
            recv_sem=recv.at[slot],
            device_id=(to, t if tp is None else tp),
            device_id_type=MESH,
        )

    loads = {
        L_B: pltpu.make_async_copy(b_hbm, bv, local.at[L_B]),
        L_C: pltpu.make_async_copy(c_hbm, cv, local.at[L_C]),
        L_X: pltpu.make_async_copy(x_hbm, xv, local.at[L_X]),
        L_Z: pltpu.make_async_copy(z_hbm, zv, local.at[L_Z]),
        L_K: pltpu.make_async_copy(k_hbm, kbuf.at[0], local.at[L_K]),
        L_V: pltpu.make_async_copy(v_hbm, vbuf.at[0], local.at[L_V]),
        L_Q: pltpu.make_async_copy(q_hbm, qv, local.at[L_Q]),
    }

    barrier = pltpu.get_barrier_semaphore()
    for source in (sib, at(-1), at(-2), upper, pass_from):
        pl.semaphore_signal(barrier, inc=1, device_id=(source, t), device_id_type=MESH)
    for step in range(1, n_tp):
        pl.semaphore_signal(
            barrier, inc=1, device_id=(p, lax.rem(t + n_tp - step, n_tp)), device_id_type=MESH
        )
    for slot in (L_B, L_C, L_X, L_Z, L_K, L_V, L_Q):
        loads[slot].start()
    pl.semaphore_wait(barrier, 5 + n_tp - 1)

    last_rows = pl.ds(TOK - 16, 16)
    rims = [
        remote(b_hbm.at[last_rows], rim_b, RIM_B, at(1)),
        remote(c_hbm.at[last_rows], rim_c, RIM_C, at(1)),
        remote(x_hbm.at[last_rows], rim_x, RIM_X, at(1)),
    ]
    for copy in rims:
        copy.start()
    near = [
        remote(v_hbm, vbuf.at[1], V1, at(2)),
        remote(k_hbm, kbuf.at[1], K1, at(2)),
    ]
    k_down = remote(k_hbm, k_pass, KZ, lower)
    far = [
        remote(vbuf.at[1], vbuf.at[3], V2, at(2)),
        remote(k_pass, kbuf.at[3], K2, pass_to),
    ]
    for copy in near:
        copy.start()
    k_down.start()
    own_to_sib = [
        remote(k_hbm, kbuf.at[4], KX, sib),
        remote(v_hbm, vbuf.at[4], VX, sib),
    ]

    @pl.when(core == 0)
    def _():
        for copy in own_to_sib:
            copy.start()

    def id_row(row):
        return ids[pl.ds(row, 1), :].astype(F32)

    def id_column(row):
        return jnp.broadcast_to(id_row(row), (128, 128)).T

    def id_columns(device):
        return jnp.concatenate([id_column(2 * device), id_column(2 * device + 1)], axis=0)

    own_cols = id_columns(p)
    own_row = jnp.concatenate([id_row(2 * p), id_row(2 * p + 1)], axis=1)
    last_id = own_row[:, TOK - 1 : TOK]
    before_row = lax.rem(2 * p - 1 + 2 * n_ctx, 2 * n_ctx)
    first_device = p == 0
    before_cols = jnp.where(first_device, -1.0, id_column(before_row))
    before_id = jnp.where(first_device, -1.0, id_row(before_row))[:, 127:128]
    lanes = lax.broadcasted_iota(jnp.int32, (TOK, 128), 1).astype(F32)
    row_at = lax.broadcasted_iota(jnp.int32, (TOK, TOK), 0)
    col_at = lax.broadcasted_iota(jnp.int32, (TOK, TOK), 1)
    same = repeat_lanes(own_cols, 2) == own_row
    causal = col_at <= row_at
    allowed = same & causal
    for back in range(1, 4):
        shift[pl.ds((back - 1) * TOK, TOK), :] = jnp.where(
            same & (row_at - col_at == back), 1.0, 0.0
        ).astype(BF16)
    tops = lax.broadcasted_iota(jnp.int32, (8, 128), 0)
    rim_keep = [
        jnp.where(
            (tops < back) & (own_cols[:8] == pltpu.roll(before_cols[120:], back, 0)), 1.0, 0.0
        )
        for back in range(1, 4)
    ]

    raw = dt_raw[...].astype(F32)
    raw = jnp.concatenate([raw, raw], axis=0).T + repeat_lanes(dt_bias[...], 2)
    steps = jnp.maximum(raw, 0.0) + jnp.log(1.0 + jnp.exp(-jnp.abs(raw)))
    log_decay = -steps * repeat_lanes(rates[...], 2)
    upto = jnp.where(causal, 1.0, 0.0).astype(BF16)
    part = log_decay.astype(BF16)
    rest = log_decay - part.astype(F32)
    part2 = rest.astype(BF16)
    part3 = (rest - part2.astype(F32)).astype(BF16)
    cum = dot(upto, part) + (dot(upto, part2) + dot(upto, part3))
    middle = cum[TOK // 2 - 1 : TOK // 2]
    end = cum[TOK - 1 : TOK]
    expand[pl.ds(0, TOK), :] = split2(jnp.exp(middle - cum) * steps)
    expand[pl.ds(TOK, TOK), :] = split2(jnp.exp(cum - middle))
    continues = before_id == last_id
    through = jnp.where(continues, jnp.exp(end), 0.0)
    t_own[...] = jnp.broadcast_to(through, (8, 128))
    t_send = remote(t_own, t_sib, T_SIB, sib)
    t_send.start()

    def spread_matrix(tile):
        head = lax.broadcasted_iota(jnp.int32, (128, WIDE), 0) & 63
        place = (lax.broadcasted_iota(jnp.int32, (128, WIDE), 1) >> 6) + tile * (WIDE // 64)
        return jnp.where(head == place, 1.0, 0.0).astype(BF16)

    def conv(source, rim, weights, width):
        moved = dot(shift[...], source)
        taps = weights.astype(F32)
        total = taps[3:4] * source.astype(F32)
        edge = jnp.zeros((8, width), F32)
        rim8 = rim.astype(F32)[8:16]
        for back in range(1, 4):
            tap = taps[3 - back : 4 - back]
            total = total + tap * moved[(back - 1) * TOK : back * TOK]
            keep = repeat_lanes(rim_keep[back - 1], width // 128)
            edge = edge + tap * (keep * pltpu.roll(rim8, back, 0))
        total = jnp.concatenate([total[:8] + edge, total[8:]], axis=0)
        return silu(total).astype(BF16)

    loads[L_B].wait()
    rims[0].wait()
    b_conv = conv(bv[...], rim_b[...], conv_b[...], bv.shape[1])
    for group in range(groups):
        b_group = b_conv[:, group * STATE : (group + 1) * STATE]
        ending = jnp.where(own_cols == last_id, b_group.astype(F32), 0.0)
        bt[group] = ending.T.astype(BF16)

    t_send.wait()
    t_chip[...] = t_own[...] * t_sib[...]
    t_next = remote(t_chip, t_n1, T_C, at(2))
    t_next.start()
    is_low = core == 0
    rows = lax.broadcasted_iota(jnp.int32, (16, 128), 0)
    vectors = jnp.where(rows == 0, jnp.exp(end - middle), 0.0)
    vectors = jnp.where(rows == 1, repeat_lanes(skip_d[...], 2), vectors)
    vectors = jnp.where(rows == 2, jnp.where(is_low, t_sib[0:1], 1.0), vectors)
    vectors = jnp.where(rows == 3, jnp.where(is_low, 1.0, t_own[0:1]), vectors)
    expand[pl.ds(2 * TOK, 16), :] = split2(vectors)

    loads[L_X].wait()
    rims[2].wait()

    def end_state(tile):
        here = pl.ds(pl.multiple_of(tile * WIDE, WIDE), WIDE)
        x_conv = conv(xv[:, here], rim_x[:, here], conv_x[:, here], WIDE)
        xv[:, here] = x_conv
        spread = spread_matrix(tile)
        factors = dot(expand[pl.ds(0, TOK), :], spread)
        vectors = dot(expand[pl.ds(2 * TOK, 16), :], spread)
        x_scaled = (x_conv.astype(F32) * factors).astype(BF16)
        xs[:, here] = x_scaled
        state = dot(bt[tile // per_group], x_scaled) * vectors[0:1]
        e_own[tile] = state.astype(BF16)
        return state, vectors

    mine, others = core * CHUNKS, (1 - core) * CHUNKS

    k_down.wait()
    far[1].start()
    halves = [
        remote(e_own.at[others + i], e_sib.at[others + i], E_A + i, sib) for i in range(CHUNKS)
    ]
    nears = [remote(e_chip.at[i], e_n1.at[i], E1 + i, at(2)) for i in range(PIECES)]
    downs = [
        None if i in FORWARD else remote(e_chip.at[i], e_pass.at[i], EZ + i, lower)
        for i in range(PIECES)
    ]
    passes = [
        remote(e_n1.at[i], e_n2.at[i], E2 + i, at(2))
        if i in FORWARD
        else remote(e_pass.at[i], e_n2.at[i], E2 + i, pass_to)
        for i in range(PIECES)
    ]

    def pass_on(*pieces):
        for i in pieces:
            (nears[i] if i in FORWARD else downs[i]).wait_recv()
            passes[i].start()

    for step in range(CHUNKS + 1):
        if step < CHUNKS:
            end_state(others + step)
            halves[step].start()
        if step == 1:
            near[0].wait()
            far[0].start()
        if step == 0:
            continue
        chunk = step - 1
        state, vectors = end_state(mine + chunk)
        halves[chunk].wait()
        chip_end = (
            vectors[2:3] * state + vectors[3:4] * e_sib[mine + chunk].astype(F32)
        ).astype(BF16)
        for i in range(WIDE // PIECE):
            piece = chunk * (WIDE // PIECE) + i
            e_chip[piece] = chip_end[:, i * PIECE : (i + 1) * PIECE]
            nears[piece].start()
            if downs[piece] is not None:
                downs[piece].start()
    half_b = remote(e_own.at[pl.ds(mine, CHUNKS)], e_sib.at[pl.ds(mine, CHUNKS)], E_B, sib)
    half_b.start()
    near[1].wait()
    sib_near = [
        remote(kbuf.at[1], kbuf.at[2], K1S, sib),
        remote(vbuf.at[1], vbuf.at[2], V1S, sib),
    ]
    for copy in sib_near:
        copy.start()

    loads[L_C].wait()
    rims[1].wait()
    c_conv = conv(cv[...], rim_c[...], conv_c[...], cv.shape[1])
    for group in range(groups):
        b_group = b_conv[:, group * STATE : (group + 1) * STATE]
        c_group = c_conv[:, group * STATE : (group + 1) * STATE]
        mix[group] = jnp.where(allowed, dot_nt(c_group, b_group), 0.0).astype(BF16)
        cj[group] = jnp.where(own_cols == before_id, c_group.astype(F32), 0.0).astype(BF16)

    far_own[...] = jnp.where(own_cols == lanes, 0.0, -FAR).astype(BF16)
    block_devices = (p, p - 2, p - 1 - 2 * core, p - 4, p - 3 + 2 * core)
    for slot, device in enumerate(block_devices):
        columns = id_columns(lax.rem(device + n_ctx, n_ctx)) if slot else own_cols
        hot[slot] = jnp.where(columns == lanes, 1.0, 0.0).astype(BF16)
    tri_bias[...] = jnp.where(causal, 0.0, -FAR)

    loads[L_Z].wait()

    def gate_tile(tile, carry):
        here = pl.ds(pl.multiple_of(tile * WIDE, WIDE), WIDE)
        spread = spread_matrix(tile)
        leaving = dot(expand[pl.ds(TOK, TOK), :], spread)
        vectors = dot(expand[pl.ds(2 * TOK, 16), :], spread)
        open_gate = silu(zv[:, here].astype(F32))
        full = leaving * dot(mix[tile // per_group], xs[:, here]) + vectors[1:2] * xv[
            :, here
        ].astype(F32)
        g1[:, here] = full * open_gate
        gate[:, here] = leaving * open_gate
        return carry

    lax.fori_loop(0, tiles // 2, gate_tile, 0, unroll=2)
    pass_on(0, 1)
    lax.fori_loop(tiles // 2, tiles, gate_tile, 0, unroll=2)
    pass_on(2, 3)

    for copy in far:
        copy.wait()
    far_to_sib = [
        remote(kbuf.at[3], kbuf.at[4], KX, sib),
        remote(vbuf.at[3], vbuf.at[4], VX, sib),
    ]

    @pl.when(core == 1)
    def _():
        for copy in far_to_sib:
            copy.start()
        for copy in far_to_sib:
            copy.wait_send()

    @pl.when(core == 0)
    def _():
        for copy in own_to_sib:
            copy.wait_send()

    for copy in far_to_sib:
        copy.wait_recv()
    for copy in sib_near:
        copy.wait()
    for slot in (L_K, L_V, L_Q):
        loads[slot].wait()

    factor = HEAD_DIM**-0.5 * LOG2E
    query_heads = q_hbm.shape[1] // HEAD_DIM
    per_kv = query_heads // (k_hbm.shape[1] // HEAD_DIM)

    def attend(head, carry):
        here = pl.ds(pl.multiple_of(head * HEAD_DIM, HEAD_DIM), HEAD_DIM)
        kv = pl.ds(pl.multiple_of((head // per_kv) * HEAD_DIM, HEAD_DIM), HEAD_DIM)
        query = jnp.concatenate([qv[:, here], far_own[...]], axis=1)
        scores = []
        for slot in range(5):
            key = jnp.concatenate([kbuf[slot, :, kv], hot[slot]], axis=1)
            scores.append(dot_nt(query, key))
        scores[0] = scores[0] + tri_bias[...]
        top = functools.reduce(jnp.maximum, scores)
        top = jnp.max(top, axis=1, keepdims=True) * factor
        ones = jnp.ones((TOK, HEAD_DIM), BF16)
        summed = jnp.zeros((TOK, 2 * HEAD_DIM), F32)
        for slot in range(5):
            weights = jnp.exp2(scores[slot] * factor - top).astype(BF16)
            value = jnp.concatenate([vbuf[slot, :, kv], ones], axis=1)
            summed = summed + dot(weights, value)
        ao[:, here] = (summed[:, :HEAD_DIM] / summed[:, HEAD_DIM:]).astype(BF16)
        return carry

    per_part = query_heads // CHUNKS

    t_next.wait()
    half_b.wait()
    vectors = jnp.where(rows == 0, jnp.where(is_low, 0.0, jnp.exp(middle)), 0.0)
    vectors = jnp.where(rows == 1, jnp.where(is_low, 1.0, t_sib[0:1]) * jnp.exp(middle), vectors)
    vectors = jnp.where(rows == 2, t_n1[0:1], vectors)
    expand_in[...] = split2(vectors)

    def spread_tile(tile, carry):
        spread_in[tile] = dot(expand_in[...], spread_matrix(tile))
        return carry

    lax.fori_loop(0, tiles, spread_tile, 0)
    sumsq[...] = jnp.zeros_like(sumsq)

    def join_tile(tile, incoming):
        here = pl.ds(pl.multiple_of(tile * WIDE, WIDE), WIDE)
        vectors = spread_in[tile]
        state = vectors[0:1] * e_sib[tile].astype(F32) + vectors[1:2] * incoming
        gated = g1[:, here] + gate[:, here] * dot(cj[tile // per_group], state.astype(BF16))
        g1[:, here] = gated
        squares = gated * gated
        total = sumsq[...]
        for lane in range(WIDE // 128):
            total = total + squares[:, lane * 128 : (lane + 1) * 128]
        sumsq[...] = total

    swaps = [remote(in_own.at[i], in_sib.at[i], IN + i, sib) for i in range(CHUNKS)]
    sq_sends = [
        remote(sq_own, sq_in.at[step - 1], SQ + step - 1, p, lax.rem(t + step, n_tp))
        for step in range(1, n_tp)
    ]

    def join_all():
        for chunk in range(CHUNKS):
            tile = mine + chunk
            pieces = range(chunk * (WIDE // PIECE), (chunk + 1) * (WIDE // PIECE))
            for i in pieces:
                if i not in FORWARD:
                    nears[i].wait_recv()
                passes[i].wait_recv()
            near_end = jnp.concatenate([e_n1[i] for i in pieces], axis=1).astype(F32)
            far_end = jnp.concatenate([e_n2[i] for i in pieces], axis=1).astype(F32)
            arriving = near_end + spread_in[tile][2:3] * far_end
            in_own[chunk] = arriving.astype(BF16)
            swaps[chunk].start()
            join_tile(tile, arriving)
        for chunk in range(CHUNKS):
            swaps[chunk].wait()
            join_tile(others + chunk, in_sib[chunk].astype(F32))

        own_sums = jnp.concatenate(
            [
                jnp.sum(sumsq[pl.ds(0, 128), :].T, axis=0, keepdims=True),
                jnp.sum(sumsq[pl.ds(128, 128), :].T, axis=0, keepdims=True),
            ],
            axis=1,
        )
        sq_own[...] = jnp.broadcast_to(own_sums, (8, TOK))
        for copy in sq_sends:
            copy.start()

    def attend_part(part, carry):
        for i in range(per_part):
            attend(part * per_part + i, carry)

        @pl.when(part == 0)
        def _():
            pass_on(4, 5)

        @pl.when(part == 1)
        def _():
            pass_on(6, 7)

        @pl.when(part == CHUNKS - 2)
        def _():
            join_all()

        return carry

    lax.fori_loop(0, CHUNKS, attend_part, 0)
    ao_out = pltpu.make_async_copy(ao, ao_hbm, local.at[L_AO])
    ao_out.start()
    for copy in sq_sends:
        copy.wait()
    for i in range(PIECES):
        nears[i].wait_send()
        passes[i].wait_send()
        if downs[i] is not None:
            downs[i].wait_send()
    total = sq_own[...]
    for step in range(1, n_tp):
        total = total + sq_in[step - 1]
    scale = lax.rsqrt(total[0:1] / INNER + EPSILON)
    scale_cols = jnp.concatenate(
        [
            jnp.broadcast_to(scale[:, :128], (128, 128)).T,
            jnp.broadcast_to(scale[:, 128:], (128, 128)).T,
        ],
        axis=0,
    )
    scale_wide = repeat_lanes(scale_cols, WIDE // 128)

    outs = []
    for tile in range(tiles):
        here = slice(tile * WIDE, (tile + 1) * WIDE)
        mo[:, here] = (g1[:, here] * scale_wide * gain[:, here]).astype(BF16)
        out = pltpu.make_async_copy(
            mo.at[:, pl.ds(tile * WIDE, WIDE)],
            mo_hbm.at[:, pl.ds(tile * WIDE, WIDE)],
            local.at[L_MO + tile],
        )
        out.start()
        outs.append(out)
    ao_out.wait()
    for out in outs:
        out.wait()


def per_device(q, k, v, ids, x, b, c, z, dt_raw, conv_x, conv_b, conv_c, dt_bias, rates, skip_d, gain):
    n_ctx, n_tp = lax.axis_size("ctx"), lax.axis_size("tp")
    channels = x.shape[1]
    tiles = channels // WIDE
    groups = b.shape[1] // STATE
    hbm = pl.BlockSpec(memory_space=pl.ANY)
    vmem = pl.BlockSpec(memory_space=pltpu.VMEM)
    specs = [hbm, hbm, hbm, vmem, hbm, hbm, hbm, hbm] + [vmem] * 8
    scratch = [
        pltpu.VMEM(x.shape, BF16),
        pltpu.VMEM(z.shape, BF16),
        pltpu.VMEM(q.shape, BF16),
        pltpu.VMEM((5,) + k.shape, BF16),
        pltpu.VMEM((5,) + v.shape, BF16),
        pltpu.VMEM(k.shape, BF16),
        pltpu.VMEM(b.shape, BF16),
        pltpu.VMEM(c.shape, BF16),
        pltpu.VMEM((16, channels), BF16),
        pltpu.VMEM((16, b.shape[1]), BF16),
        pltpu.VMEM((16, c.shape[1]), BF16),
        pltpu.VMEM(x.shape, BF16),
        pltpu.VMEM(x.shape, F32),
        pltpu.VMEM(x.shape, F32),
        pltpu.VMEM((tiles, STATE, WIDE), BF16),
        pltpu.VMEM((tiles, STATE, WIDE), BF16),
        pltpu.VMEM((PIECES, STATE, PIECE), BF16),
        pltpu.VMEM((PIECES, STATE, PIECE), BF16),
        pltpu.VMEM((PIECES, STATE, PIECE), BF16),
        pltpu.VMEM((PIECES, STATE, PIECE), BF16),
        pltpu.VMEM((CHUNKS, STATE, WIDE), BF16),
        pltpu.VMEM((CHUNKS, STATE, WIDE), BF16),
        pltpu.VMEM((8, 128), F32),
        pltpu.VMEM((8, 128), F32),
        pltpu.VMEM((8, 128), F32),
        pltpu.VMEM((8, 128), F32),
        pltpu.VMEM((8, TOK), F32),
        pltpu.VMEM((n_tp - 1, 8, TOK), F32),
        pltpu.VMEM((2 * TOK + 16, 128), BF16),
        pltpu.VMEM((16, 128), BF16),
        pltpu.VMEM((tiles, 16, WIDE), F32),
        pltpu.VMEM((3 * TOK, TOK), BF16),
        pltpu.VMEM((groups, TOK, TOK), BF16),
        pltpu.VMEM((groups, STATE, TOK), BF16),
        pltpu.VMEM((groups, TOK, STATE), BF16),
        pltpu.VMEM((TOK, 128), BF16),
        pltpu.VMEM((5, TOK, 128), BF16),
        pltpu.VMEM((TOK, TOK), F32),
        pltpu.VMEM(q.shape, BF16),
        pltpu.VMEM(x.shape, BF16),
        pltpu.VMEM((TOK, 128), F32),
        pltpu.SemaphoreType.DMA((COPIES,)),
        pltpu.SemaphoreType.DMA((COPIES,)),
        pltpu.SemaphoreType.DMA((L_MO + tiles,)),
    ]
    return pl.pallas_call(
        functools.partial(kernel, n_ctx, n_tp),
        out_shape=(
            jax.ShapeDtypeStruct(q.shape, BF16),
            jax.ShapeDtypeStruct(x.shape, BF16),
        ),
        in_specs=specs,
        out_specs=(hbm, hbm),
        scratch_shapes=scratch,
        compiler_params=pltpu.CompilerParams(
            collective_id=1, has_side_effects=True, vmem_limit_bytes=56 * 2**20
        ),
        name="packed_mix",
    )(
        q,
        k,
        v,
        ids.reshape(-1, 128),
        x,
        b,
        c,
        z,
        dt_raw.T,
        conv_x,
        conv_b,
        conv_c,
        dt_bias[None],
        rates[None],
        skip_d[None],
        gain[None],
    )


def solution(mesh):
    both = P("ctx", "tp")
    placed = (both, both, both, P(), both, both, both, both, both)
    placed += (P(None, "tp"),) * 3 + (P("tp"),) * 4
    return jax.shard_map(
        per_device, mesh=mesh, in_specs=placed, out_specs=(both, both), check_vma=False
    )
```

```python
import functools

import jax
import jax.numpy as jnp
from jax import lax
from jax.experimental import pallas as pl
from jax.experimental.pallas import tpu as pltpu
from jax.sharding import PartitionSpec as P

HEAD_DIM = 128
STATE = 128
INNER = 16384
EPSILON = 1e-05
FAR = 1e30
LOG2E = 1.4426950408889634

TOK = 256
WIDE = 512
PARTS = 4
Z_CHIPS = 4
MESH = pl.DeviceIdType.MESH
F32 = jnp.float32
BF16 = jnp.bfloat16

CHUNKS = 4
PIECE = 256
PIECES = CHUNKS * WIDE // PIECE
RIM_X, RIM_B, RIM_C, K1, V1, KZ, K2, V2, KX, VX, K1S, V1S, E_B, T_SIB, T_C = range(15)
E_A = 15
E1 = E_A + CHUNKS
EZ = E1 + PIECES
E2 = EZ + PIECES
IN = E2 + PIECES
SQ = IN + CHUNKS
COPIES = SQ + 3
L_R, L_X, L_Z, L_Q, L_K, L_V, L_B, L_C, L_AO, L_SCALE, L_GATED = range(11)


def dot(a, b):
    return lax.dot_general(a, b, (((1,), (0,)), ((), ())), preferred_element_type=F32)


def dot_nt(a, b):
    return lax.dot_general(a, b, (((1,), (1,)), ((), ())), preferred_element_type=F32)


def silu(a):
    half = 0.5 * a
    return half + half * jnp.tanh(half)


def repeat_lanes(a, times):
    return jnp.concatenate([a] * times, axis=1)


def split2(a):
    high = a.astype(BF16).astype(F32)
    lane = lax.broadcasted_iota(jnp.int32, a.shape, 1)
    return jnp.where(lane < 64, high, a - high).astype(BF16)


def kernel(
    n_ctx,
    n_tp,
    q_hbm,
    k_hbm,
    v_hbm,
    ids,
    x_hbm,
    b_hbm,
    c_hbm,
    z_hbm,
    dt_raw,
    conv_x,
    conv_b,
    conv_c,
    dt_bias,
    rates,
    skip_d,
    ao_hbm,
    gated_hbm,
    scale_hbm,
    xv,
    zv,
    qv,
    kbuf,
    vbuf,
    k_pass,
    bv,
    cv,
    x_end,
    x_ends,
    rim_x,
    rim_b,
    rim_c,
    xs,
    g1,
    gate,
    e_own,
    e_sib,
    e_chip,
    e_n1,
    e_n2,
    e_pass,
    e_pair,
    chip_decay,
    in_own,
    in_sib,
    t_own,
    t_sib,
    t_chip,
    t_n1,
    sq_own,
    sq_in,
    expand,
    expand_in,
    spread_in,
    shift,
    mix,
    bt,
    cj,
    far_own,
    hot,
    tri_bias,
    ao,
    gated_out,
    scale_out,
    sumsq,
    send,
    recv,
    local,
):
    p = lax.axis_index("ctx")
    t = lax.axis_index("tp")
    core = lax.rem(p, 2)
    sib = p + 1 - 2 * core
    channels = x_hbm.shape[1]
    groups = bv.shape[1] // STATE
    tiles = channels // WIDE
    per_group = tiles // groups
    chip = p // 2
    x_at, z_at = chip // Z_CHIPS, lax.rem(chip, Z_CHIPS)
    x_chips = n_ctx // (2 * Z_CHIPS)

    def chip_device(x, z):
        return (lax.rem(x, x_chips) * Z_CHIPS + lax.rem(z, Z_CHIPS)) * 2 + core

    wraps = ((z_at == 1) | (z_at == 2)).astype(jnp.int32)
    pass_to = chip_device(x_at + wraps, z_at + Z_CHIPS - 1)
    lower = chip_device(x_at, z_at + Z_CHIPS - 1)
    upper = chip_device(x_at, z_at + 1)
    upper_wraps = ((z_at == 0) | (z_at == 1)).astype(jnp.int32)
    pass_from = chip_device(x_at + x_chips - upper_wraps, z_at + 1)

    def at(offset):
        return lax.rem(p + offset + n_ctx, n_ctx)

    def remote(src, dst, slot, to, tp=None):
        return pltpu.make_async_remote_copy(
            src_ref=src,
            dst_ref=dst,
            send_sem=send.at[slot],
            recv_sem=recv.at[slot],
            device_id=(to, t if tp is None else tp),
            device_id_type=MESH,
        )

    last_rows = pl.ds(TOK - 16, 16)
    loads = {
        L_R: pltpu.make_async_copy(x_hbm.at[last_rows], x_end, local.at[L_R]),
        L_B: pltpu.make_async_copy(b_hbm, bv, local.at[L_B]),
        L_C: pltpu.make_async_copy(c_hbm, cv, local.at[L_C]),
        L_X: pltpu.make_async_copy(x_hbm, xv, local.at[L_X]),
        L_Z: pltpu.make_async_copy(z_hbm, zv, local.at[L_Z]),
        L_K: pltpu.make_async_copy(k_hbm, kbuf.at[0], local.at[L_K]),
        L_V: pltpu.make_async_copy(v_hbm, vbuf.at[0], local.at[L_V]),
        L_Q: pltpu.make_async_copy(q_hbm, qv, local.at[L_Q]),
    }

    barrier = pltpu.get_barrier_semaphore()
    for source in (sib, at(-1), at(-2), upper, pass_from):
        pl.semaphore_signal(barrier, inc=1, device_id=(source, t), device_id_type=MESH)
    for step in range(1, n_tp):
        pl.semaphore_signal(
            barrier, inc=1, device_id=(p, lax.rem(t + n_tp - step, n_tp)), device_id_type=MESH
        )
    for slot in (L_R, L_B, L_C, L_X, L_Z, L_K, L_V, L_Q):
        loads[slot].start()
    loads[L_R].wait()
    eighth = lax.broadcasted_iota(jnp.int32, (8, WIDE), 0)
    for block in range(tiles // 4):
        ends = [
            x_end[:, (4 * block + i) * WIDE : (4 * block + i + 1) * WIDE].astype(F32)[8:]
            for i in range(4)
        ]
        pairs = [
            jnp.where(eighth < 4, pltpu.roll(ends[i], 4, 0), ends[i + 1]) for i in (0, 2)
        ]
        x_ends[block] = jnp.concatenate(pairs, axis=0).astype(BF16)
    pl.semaphore_wait(barrier, 5 + n_tp - 1)

    rims = [
        remote(b_hbm.at[last_rows], rim_b, RIM_B, at(1)),
        remote(c_hbm.at[last_rows], rim_c, RIM_C, at(1)),
        remote(x_ends, rim_x, RIM_X, at(1)),
    ]
    for copy in rims:
        copy.start()
    near = [
        remote(v_hbm, vbuf.at[1], V1, at(2)),
        remote(k_hbm, kbuf.at[1], K1, at(2)),
    ]
    k_down = remote(k_hbm, k_pass, KZ, lower)
    far = [
        remote(vbuf.at[1], vbuf.at[3], V2, at(2)),
        remote(k_pass, kbuf.at[3], K2, pass_to),
    ]
    for copy in near:
        copy.start()
    k_down.start()
    own_to_sib = [
        remote(k_hbm, kbuf.at[4], KX, sib),
        remote(v_hbm, vbuf.at[4], VX, sib),
    ]

    @pl.when(core == 0)
    def _():
        for copy in own_to_sib:
            copy.start()

    def id_row(row):
        return ids[pl.ds(row, 1), :].astype(F32)

    def id_column(row):
        return jnp.broadcast_to(id_row(row), (128, 128)).T

    def id_columns(device):
        return jnp.concatenate([id_column(2 * device), id_column(2 * device + 1)], axis=0)

    own_cols = id_columns(p)
    own_row = jnp.concatenate([id_row(2 * p), id_row(2 * p + 1)], axis=1)
    last_id = own_row[:, TOK - 1 : TOK]
    before_row = lax.rem(2 * p - 1 + 2 * n_ctx, 2 * n_ctx)
    first_device = p == 0
    before_cols = jnp.where(first_device, -1.0, id_column(before_row))
    before_id = jnp.where(first_device, -1.0, id_row(before_row))[:, 127:128]
    lanes = lax.broadcasted_iota(jnp.int32, (TOK, 128), 1).astype(F32)
    row_at = lax.broadcasted_iota(jnp.int32, (TOK, TOK), 0)
    col_at = lax.broadcasted_iota(jnp.int32, (TOK, TOK), 1)
    same = repeat_lanes(own_cols, 2) == own_row
    causal = col_at <= row_at
    allowed = same & causal
    for back in range(1, 4):
        shift[pl.ds((back - 1) * TOK, TOK), :] = jnp.where(
            same & (row_at - col_at == back), 1.0, 0.0
        ).astype(BF16)
    tops = lax.broadcasted_iota(jnp.int32, (8, 128), 0)
    rim_keep = [
        jnp.where(
            (tops < back) & (own_cols[:8] == pltpu.roll(before_cols[120:], back, 0)), 1.0, 0.0
        )
        for back in range(1, 4)
    ]

    raw = dt_raw[...].astype(F32)
    raw = jnp.concatenate([raw, raw], axis=0).T + repeat_lanes(dt_bias[...], 2)
    steps = jnp.maximum(raw, 0.0) + jnp.log(1.0 + jnp.exp(-jnp.abs(raw)))
    log_decay = -steps * repeat_lanes(rates[...], 2)
    upto = jnp.where(causal, 1.0, 0.0).astype(BF16)
    part = log_decay.astype(BF16)
    rest = log_decay - part.astype(F32)
    part2 = rest.astype(BF16)
    part3 = (rest - part2.astype(F32)).astype(BF16)
    cum = dot(upto, part) + (dot(upto, part2) + dot(upto, part3))
    middle = cum[TOK // 2 - 1 : TOK // 2]
    end = cum[TOK - 1 : TOK]
    expand[pl.ds(0, TOK), :] = split2(jnp.exp(middle - cum) * steps)
    expand[pl.ds(TOK, TOK), :] = split2(jnp.exp(cum - middle))
    continues = before_id == last_id
    through = jnp.where(continues, jnp.exp(end), 0.0)
    t_own[...] = jnp.broadcast_to(through, (8, 128))
    t_send = remote(t_own, t_sib, T_SIB, sib)
    t_send.start()

    def spread_matrix(tile):
        head = lax.broadcasted_iota(jnp.int32, (128, WIDE), 0) & 63
        place = (lax.broadcasted_iota(jnp.int32, (128, WIDE), 1) >> 6) + tile * (WIDE // 64)
        return jnp.where(head == place, 1.0, 0.0).astype(BF16)

    def conv(source, rim8, weights, width):
        moved = dot(shift[...], source)
        taps = weights.astype(F32)
        total = taps[3:4] * source.astype(F32)
        edge = jnp.zeros((8, width), F32)
        for back in range(1, 4):
            tap = taps[3 - back : 4 - back]
            total = total + tap * moved[(back - 1) * TOK : back * TOK]
            keep = repeat_lanes(rim_keep[back - 1], width // 128)
            edge = edge + tap * (keep * pltpu.roll(rim8, back, 0))
        total = jnp.concatenate([total[:8] + edge, total[8:]], axis=0)
        return silu(total).astype(BF16)

    loads[L_B].wait()
    rims[0].wait()
    b_conv = conv(bv[...], rim_b[...].astype(F32)[8:], conv_b[...], bv.shape[1])
    for group in range(groups):
        b_group = b_conv[:, group * STATE : (group + 1) * STATE]
        ending = jnp.where(own_cols == last_id, b_group.astype(F32), 0.0)
        bt[group] = ending.T.astype(BF16)

    t_send.wait()
    t_chip[...] = t_own[...] * t_sib[...]
    t_next = remote(t_chip, t_n1, T_C, at(2))
    t_next.start()
    is_low = core == 0
    rows = lax.broadcasted_iota(jnp.int32, (16, 128), 0)
    vectors = jnp.where(rows == 0, jnp.exp(end - middle), 0.0)
    vectors = jnp.where(rows == 1, repeat_lanes(skip_d[...], 2), vectors)
    vectors = jnp.where(rows == 2, jnp.where(is_low, t_sib[0:1], 1.0), vectors)
    vectors = jnp.where(rows == 3, jnp.where(is_low, 1.0, t_own[0:1]), vectors)
    vectors = jnp.where(rows == 4, t_chip[0:1], vectors)
    expand[pl.ds(2 * TOK, 16), :] = split2(vectors)

    loads[L_X].wait()
    rims[2].wait()

    def end_state(first, chunk):
        tile = first + chunk
        here = pl.ds(pl.multiple_of(tile * WIDE, WIDE), WIDE)
        pair = rim_x[first // 4].astype(F32)[8 * (chunk // 2) : 8 * (chunk // 2) + 8]
        rim8 = pltpu.roll(pair, 4, 0) if chunk % 2 == 0 else pair
        x_conv = conv(xv[:, here], rim8, conv_x[:, here], WIDE)
        xv[:, here] = x_conv
        spread = spread_matrix(tile)
        factors = dot(expand[pl.ds(0, TOK), :], spread)
        vectors = dot(expand[pl.ds(2 * TOK, 16), :], spread)
        x_scaled = (x_conv.astype(F32) * factors).astype(BF16)
        xs[:, here] = x_scaled
        state = dot(bt[tile // per_group], x_scaled) * vectors[0:1]
        e_own[tile] = state.astype(BF16)
        return state, vectors

    mine, others = core * CHUNKS, (1 - core) * CHUNKS

    k_down.wait()
    far[1].start()
    halves = [
        remote(e_own.at[others + i], e_sib.at[others + i], E_A + i, sib) for i in range(CHUNKS)
    ]
    odd = lax.rem(z_at, 2) == 1
    firsts = [remote(e_chip.at[i], e_n1.at[i], E1 + i, at(2)) for i in range(PIECES)]
    pairs = [remote(e_pair.at[i], e_n1.at[i], E1 + i, at(2)) for i in range(PIECES)]
    downs = [remote(e_chip.at[i], e_pass.at[i], EZ + i, lower) for i in range(PIECES)]
    passes = [remote(e_pass.at[i], e_n2.at[i], E2 + i, pass_to) for i in range(PIECES)]

    def pass_on(*pieces):
        @pl.when(odd)
        def _():
            for i in pieces:
                chunk, lane = divmod(i * PIECE, WIDE)
                firsts[i].wait_recv()
                e_pair[i] = (
                    e_chip[i].astype(F32)
                    + chip_decay[chunk, 4:5, lane : lane + PIECE] * e_n1[i].astype(F32)
                ).astype(BF16)
                pairs[i].start()

        @pl.when(jnp.logical_not(odd))
        def _():
            for i in pieces:
                downs[i].wait_recv()
                passes[i].start()

    for step in range(CHUNKS + 1):
        if step < CHUNKS:
            end_state(others, step)
            halves[step].start()
        if step == 1:
            near[0].wait()
            far[0].start()
        if step == 0:
            continue
        chunk = step - 1
        state, vectors = end_state(mine, chunk)
        chip_decay[chunk] = vectors[:8]
        halves[chunk].wait()
        chip_end = (
            vectors[2:3] * state + vectors[3:4] * e_sib[mine + chunk].astype(F32)
        ).astype(BF16)
        for i in range(WIDE // PIECE):
            piece = chunk * (WIDE // PIECE) + i
            e_chip[piece] = chip_end[:, i * PIECE : (i + 1) * PIECE]

            @pl.when(odd)
            def _():
                downs[piece].start()

            @pl.when(jnp.logical_not(odd))
            def _():
                firsts[piece].start()

    half_b = remote(e_own.at[pl.ds(mine, CHUNKS)], e_sib.at[pl.ds(mine, CHUNKS)], E_B, sib)
    half_b.start()
    near[1].wait()
    sib_near = [
        remote(kbuf.at[1], kbuf.at[2], K1S, sib),
        remote(vbuf.at[1], vbuf.at[2], V1S, sib),
    ]
    for copy in sib_near:
        copy.start()

    loads[L_C].wait()
    rims[1].wait()
    c_conv = conv(cv[...], rim_c[...].astype(F32)[8:], conv_c[...], cv.shape[1])
    for group in range(groups):
        b_group = b_conv[:, group * STATE : (group + 1) * STATE]
        c_group = c_conv[:, group * STATE : (group + 1) * STATE]
        mix[group] = jnp.where(allowed, dot_nt(c_group, b_group), 0.0).astype(BF16)
        cj[group] = jnp.where(own_cols == before_id, c_group.astype(F32), 0.0).astype(BF16)

    far_own[...] = jnp.where(own_cols == lanes, 0.0, -FAR).astype(BF16)
    block_devices = (p, p - 2, p - 1 - 2 * core, p - 4, p - 3 + 2 * core)
    for slot, device in enumerate(block_devices):
        columns = id_columns(lax.rem(device + n_ctx, n_ctx)) if slot else own_cols
        hot[slot] = jnp.where(columns == lanes, 1.0, 0.0).astype(BF16)
    tri_bias[...] = jnp.where(causal, 0.0, -FAR)

    loads[L_Z].wait()

    def gate_tile(tile, carry):
        here = pl.ds(pl.multiple_of(tile * WIDE, WIDE), WIDE)
        spread = spread_matrix(tile)
        leaving = dot(expand[pl.ds(TOK, TOK), :], spread)
        vectors = dot(expand[pl.ds(2 * TOK, 16), :], spread)
        open_gate = silu(zv[:, here].astype(F32))
        full = leaving * dot(mix[tile // per_group], xs[:, here]) + vectors[1:2] * xv[
            :, here
        ].astype(F32)
        g1[:, here] = full * open_gate
        gate[:, here] = leaving * open_gate
        return carry

    lax.fori_loop(0, tiles, gate_tile, 0, unroll=2)
    pass_on(0, 1)

    for copy in far:
        copy.wait()
    far_to_sib = [
        remote(kbuf.at[3], kbuf.at[4], KX, sib),
        remote(vbuf.at[3], vbuf.at[4], VX, sib),
    ]

    @pl.when(core == 1)
    def _():
        for copy in far_to_sib:
            copy.start()
        for copy in far_to_sib:
            copy.wait_send()

    @pl.when(core == 0)
    def _():
        for copy in own_to_sib:
            copy.wait_send()

    for copy in far_to_sib:
        copy.wait_recv()
    for copy in sib_near:
        copy.wait()
    for slot in (L_K, L_V, L_Q):
        loads[slot].wait()

    pass_on(2, 3)

    factor = HEAD_DIM**-0.5 * LOG2E
    query_heads = q_hbm.shape[1] // HEAD_DIM
    per_kv = query_heads // (k_hbm.shape[1] // HEAD_DIM)

    def places(head):
        here = pl.ds(pl.multiple_of(head * HEAD_DIM, HEAD_DIM), HEAD_DIM)
        kv = pl.ds(pl.multiple_of((head // per_kv) * HEAD_DIM, HEAD_DIM), HEAD_DIM)
        return here, kv

    def score(head):
        here, kv = places(head)
        query = jnp.concatenate([qv[:, here], far_own[...]], axis=1)
        scores = []
        for slot in range(5):
            key = jnp.concatenate([kbuf[slot, :, kv], hot[slot]], axis=1)
            scores.append(dot_nt(query, key))
        scores[0] = scores[0] + tri_bias[...]
        return scores

    def attend(head, scores):
        here, kv = places(head)
        top = functools.reduce(jnp.maximum, scores)
        top = jnp.max(top, axis=1, keepdims=True) * factor
        ones = jnp.ones((TOK, HEAD_DIM), BF16)
        summed = jnp.zeros((TOK, 2 * HEAD_DIM), F32)
        for slot in range(5):
            weights = jnp.exp2(scores[slot] * factor - top).astype(BF16)
            value = jnp.concatenate([vbuf[slot, :, kv], ones], axis=1)
            summed = summed + dot(weights, value)
        ao[:, here] = (summed[:, :HEAD_DIM] / summed[:, HEAD_DIM:]).astype(BF16)

    per_part = query_heads // CHUNKS

    t_next.wait()
    half_b.wait()
    vectors = jnp.where(rows == 0, jnp.where(is_low, 0.0, jnp.exp(middle)), 0.0)
    vectors = jnp.where(rows == 1, jnp.where(is_low, 1.0, t_sib[0:1]) * jnp.exp(middle), vectors)
    vectors = jnp.where(rows == 2, t_n1[0:1], vectors)
    expand_in[...] = split2(vectors)

    def spread_tile(tile, carry):
        spread_in[tile] = dot(expand_in[...], spread_matrix(tile))
        return carry

    lax.fori_loop(0, tiles, spread_tile, 0)
    sumsq[...] = jnp.zeros_like(sumsq)

    def out_copy(tile, here):
        return pltpu.make_async_copy(
            gated_out.at[:, here], gated_hbm.at[:, here], local.at[L_GATED + tile]
        )

    def join_tile(tile, incoming):
        here = pl.ds(pl.multiple_of(tile * WIDE, WIDE), WIDE)
        vectors = spread_in[tile]
        state = vectors[0:1] * e_sib[tile].astype(F32) + vectors[1:2] * incoming
        gated = g1[:, here] + gate[:, here] * dot(cj[tile // per_group], state.astype(BF16))
        gated_out[:, here] = gated.astype(BF16)
        out_copy(tile, here).start()
        squares = gated * gated
        total = sumsq[...]
        for lane in range(WIDE // 128):
            total = total + squares[:, lane * 128 : (lane + 1) * 128]
        sumsq[...] = total

    swaps = [remote(in_own.at[i], in_sib.at[i], IN + i, sib) for i in range(CHUNKS)]
    sq_sends = [
        remote(sq_own, sq_in.at[step - 1], SQ + step - 1, p, lax.rem(t + step, n_tp))
        for step in range(1, n_tp)
    ]

    def join_all():
        for chunk in range(CHUNKS):
            tile = mine + chunk
            pieces = range(chunk * (WIDE // PIECE), (chunk + 1) * (WIDE // PIECE))

            @pl.when(odd)
            def _():
                for i in pieces:
                    passes[i].wait_recv()
                near_end = jnp.concatenate([e_n1[i] for i in pieces], axis=1).astype(F32)
                far_end = jnp.concatenate([e_n2[i] for i in pieces], axis=1).astype(F32)
                in_own[chunk] = (near_end + spread_in[tile][2:3] * far_end).astype(BF16)

            @pl.when(jnp.logical_not(odd))
            def _():
                for i in pieces:
                    firsts[i].wait_recv()
                in_own[chunk] = jnp.concatenate([e_n1[i] for i in pieces], axis=1)

            swaps[chunk].start()
            join_tile(tile, in_own[chunk].astype(F32))
        for chunk in range(CHUNKS):
            swaps[chunk].wait()
            join_tile(others + chunk, in_sib[chunk].astype(F32))

        own_sums = jnp.concatenate(
            [
                jnp.sum(sumsq[pl.ds(0, 128), :].T, axis=0, keepdims=True),
                jnp.sum(sumsq[pl.ds(128, 128), :].T, axis=0, keepdims=True),
            ],
            axis=1,
        )
        sq_own[...] = jnp.broadcast_to(own_sums, (8, TOK))
        for copy in sq_sends:
            copy.start()

    def attend_part(part, carry):
        first = part * per_part
        following = score(first)
        for i in range(per_part):
            scores = following
            if i + 1 < per_part:
                following = score(first + i + 1)
            attend(first + i, scores)

        @pl.when(part == 0)
        def _():
            pass_on(4, 5)

        @pl.when(part == 1)
        def _():
            pass_on(6, 7)

        @pl.when(part == CHUNKS - 2)
        def _():
            join_all()

        return carry

    lax.fori_loop(0, CHUNKS, attend_part, 0)
    ao_out = pltpu.make_async_copy(ao, ao_hbm, local.at[L_AO])
    ao_out.start()
    for copy in sq_sends:
        copy.wait()

    @pl.when(odd)
    def _():
        for i in range(PIECES):
            downs[i].wait_send()
            pairs[i].wait_send()

    @pl.when(jnp.logical_not(odd))
    def _():
        for i in range(PIECES):
            firsts[i].wait_send()
            passes[i].wait_send()

    total = sq_own[...]
    for step in range(1, n_tp):
        total = total + sq_in[step - 1]
    scale = lax.rsqrt(total[0:1] / INNER + EPSILON)
    scale_cols = jnp.concatenate(
        [
            jnp.broadcast_to(scale[:, :128], (128, 128)).T,
            jnp.broadcast_to(scale[:, 128:], (128, 128)).T,
        ],
        axis=0,
    )
    scale_out[...] = scale_cols
    scale_copy = pltpu.make_async_copy(scale_out, scale_hbm, local.at[L_SCALE])
    scale_copy.start()
    ao_out.wait()
    for tile in range(tiles):
        out_copy(tile, pl.ds(tile * WIDE, WIDE)).wait()
    scale_copy.wait()


def finish(ao_hbm, gated_hbm, scale_hbm, gain_hbm, ao_out, mo_out, ao, gated, scale, gain, mo, sems):
    parts = PARTS
    rows = TOK // parts
    scale_in = pltpu.make_async_copy(scale_hbm, scale, sems.at[0])
    gain_in = pltpu.make_async_copy(gain_hbm, gain, sems.at[1])
    ao_in = pltpu.make_async_copy(ao_hbm, ao, sems.at[2])
    ao_back = pltpu.make_async_copy(ao, ao_out, sems.at[3])

    def part(i):
        return pl.ds(i * rows, rows)

    ins = [
        pltpu.make_async_copy(gated_hbm.at[part(i)], gated.at[part(i)], sems.at[4 + i])
        for i in range(parts)
    ]
    outs = [
        pltpu.make_async_copy(mo.at[part(i)], mo_out.at[part(i)], sems.at[4 + parts + i])
        for i in range(parts)
    ]
    for copy in [scale_in, gain_in, ins[0], ao_in] + ins[1:]:
        copy.start()
    scale_in.wait()
    gain_in.wait()
    for i in range(parts):
        ins[i].wait()
        wide = repeat_lanes(scale[part(i), :], gated.shape[1] // 128)
        mo[part(i), :] = (gated[part(i), :].astype(F32) * wide * gain[...]).astype(BF16)
        outs[i].start()
        if i == 0:
            ao_in.wait()
            ao_back.start()
    ao_back.wait()
    for copy in outs:
        copy.wait()


def per_device(q, k, v, ids, x, b, c, z, dt_raw, conv_x, conv_b, conv_c, dt_bias, rates, skip_d, gain):
    n_ctx, n_tp = lax.axis_size("ctx"), lax.axis_size("tp")
    channels = x.shape[1]
    tiles = channels // WIDE
    groups = b.shape[1] // STATE
    hbm = pl.BlockSpec(memory_space=pl.ANY)
    vmem = pl.BlockSpec(memory_space=pltpu.VMEM)
    specs = [hbm, hbm, hbm, vmem, hbm, hbm, hbm, hbm] + [vmem] * 7
    scratch = [
        pltpu.VMEM(x.shape, BF16),
        pltpu.VMEM(z.shape, BF16),
        pltpu.VMEM(q.shape, BF16),
        pltpu.VMEM((5,) + k.shape, BF16),
        pltpu.VMEM((5,) + v.shape, BF16),
        pltpu.VMEM(k.shape, BF16),
        pltpu.VMEM(b.shape, BF16),
        pltpu.VMEM(c.shape, BF16),
        pltpu.VMEM((16, channels), BF16),
        pltpu.VMEM((tiles // 4, 16, WIDE), BF16),
        pltpu.VMEM((tiles // 4, 16, WIDE), BF16),
        pltpu.VMEM((16, b.shape[1]), BF16),
        pltpu.VMEM((16, c.shape[1]), BF16),
        pltpu.VMEM(x.shape, BF16),
        pltpu.VMEM(x.shape, F32),
        pltpu.VMEM(x.shape, F32),
        pltpu.VMEM((tiles, STATE, WIDE), BF16),
        pltpu.VMEM((tiles, STATE, WIDE), BF16),
        pltpu.VMEM((PIECES, STATE, PIECE), BF16),
        pltpu.VMEM((PIECES, STATE, PIECE), BF16),
        pltpu.VMEM((PIECES, STATE, PIECE), BF16),
        pltpu.VMEM((PIECES, STATE, PIECE), BF16),
        pltpu.VMEM((PIECES, STATE, PIECE), BF16),
        pltpu.VMEM((CHUNKS, 8, WIDE), F32),
        pltpu.VMEM((CHUNKS, STATE, WIDE), BF16),
        pltpu.VMEM((CHUNKS, STATE, WIDE), BF16),
        pltpu.VMEM((8, 128), F32),
        pltpu.VMEM((8, 128), F32),
        pltpu.VMEM((8, 128), F32),
        pltpu.VMEM((8, 128), F32),
        pltpu.VMEM((8, TOK), F32),
        pltpu.VMEM((n_tp - 1, 8, TOK), F32),
        pltpu.VMEM((2 * TOK + 16, 128), BF16),
        pltpu.VMEM((16, 128), BF16),
        pltpu.VMEM((tiles, 16, WIDE), F32),
        pltpu.VMEM((3 * TOK, TOK), BF16),
        pltpu.VMEM((groups, TOK, TOK), BF16),
        pltpu.VMEM((groups, STATE, TOK), BF16),
        pltpu.VMEM((groups, TOK, STATE), BF16),
        pltpu.VMEM((TOK, 128), BF16),
        pltpu.VMEM((5, TOK, 128), BF16),
        pltpu.VMEM((TOK, TOK), F32),
        pltpu.VMEM(q.shape, BF16),
        pltpu.VMEM(x.shape, BF16),
        pltpu.VMEM((TOK, 128), F32),
        pltpu.VMEM((TOK, 128), F32),
        pltpu.SemaphoreType.DMA((COPIES,)),
        pltpu.SemaphoreType.DMA((COPIES,)),
        pltpu.SemaphoreType.DMA((L_GATED + tiles,)),
    ]
    ao, gated, scale = pl.pallas_call(
        functools.partial(kernel, n_ctx, n_tp),
        out_shape=(
            jax.ShapeDtypeStruct(q.shape, BF16),
            jax.ShapeDtypeStruct(x.shape, BF16),
            jax.ShapeDtypeStruct((TOK, 128), F32),
        ),
        in_specs=specs,
        out_specs=(hbm, hbm, hbm),
        scratch_shapes=scratch,
        compiler_params=pltpu.CompilerParams(
            collective_id=1, has_side_effects=True, vmem_limit_bytes=56 * 2**20
        ),
        name="packed_mix",
    )(
        q,
        k,
        v,
        ids.reshape(-1, 128),
        x,
        b,
        c,
        z,
        dt_raw.T,
        conv_x,
        conv_b,
        conv_c,
        dt_bias[None],
        rates[None],
        skip_d[None],
    )
    return pl.pallas_call(
        finish,
        out_shape=(
            jax.ShapeDtypeStruct(q.shape, BF16),
            jax.ShapeDtypeStruct(x.shape, BF16),
        ),
        in_specs=[hbm] * 4,
        out_specs=(hbm, hbm),
        scratch_shapes=[
            pltpu.VMEM(q.shape, BF16),
            pltpu.VMEM(x.shape, BF16),
            pltpu.VMEM((TOK, 128), F32),
            pltpu.VMEM((1, channels), F32),
            pltpu.VMEM(x.shape, BF16),
            pltpu.SemaphoreType.DMA((4 + 2 * PARTS,)),
        ],
        compiler_params=pltpu.CompilerParams(vmem_limit_bytes=60 * 2**20),
        name="scale_rows",
    )(ao, gated, scale, gain[None])


def solution(mesh):
    both = P("ctx", "tp")
    placed = (both, both, both, P(), both, both, both, both, both)
    placed += (P(None, "tp"),) * 3 + (P("tp"),) * 4
    return jax.shard_map(
        per_device, mesh=mesh, in_specs=placed, out_specs=(both, both), check_vma=False
    )
```

```python
import functools

import jax
import jax.numpy as jnp
from jax import lax
from jax.experimental import pallas as pl
from jax.experimental.pallas import tpu as pltpu
from jax.sharding import PartitionSpec as P

HEAD_DIM = 128
STATE = 128
INNER = 16384
EPSILON = 1e-05
FAR = 1e30
LOG2E = 1.4426950408889634

TOK = 256
WIDE = 512
PARTS = 4
Z_CHIPS = 4
MESH = pl.DeviceIdType.MESH
F32 = jnp.float32
BF16 = jnp.bfloat16

CHUNKS = 4
PIECE = 256
PIECES = CHUNKS * WIDE // PIECE
RIM_X, RIM_B, RIM_C, K1, V1, KZ, K2, V2, KX, VX, K1S, V1S, E_B, T_SIB, T_C = range(15)
E_A = 15
E1 = E_A + CHUNKS
EZ = E1 + PIECES
E2 = EZ + PIECES
IN = E2 + PIECES
SQ = IN + CHUNKS
COPIES = SQ + 3
L_R, L_X, L_Z, L_Q, L_K, L_V, L_B, L_C, L_AO, L_SCALE, L_GATED = range(11)


def dot(a, b):
    return lax.dot_general(a, b, (((1,), (0,)), ((), ())), preferred_element_type=F32)


def dot_nt(a, b):
    return lax.dot_general(a, b, (((1,), (1,)), ((), ())), preferred_element_type=F32)


def silu(a):
    half = 0.5 * a
    return half + half * jnp.tanh(half)


def repeat_lanes(a, times):
    return jnp.concatenate([a] * times, axis=1)


def split2(a):
    high = a.astype(BF16).astype(F32)
    lane = lax.broadcasted_iota(jnp.int32, a.shape, 1)
    return jnp.where(lane < 64, high, a - high).astype(BF16)


def kernel(
    n_ctx,
    n_tp,
    q_hbm,
    k_hbm,
    v_hbm,
    ids,
    x_hbm,
    b_hbm,
    c_hbm,
    z_hbm,
    dt_raw,
    conv_x,
    conv_b,
    conv_c,
    dt_bias,
    rates,
    skip_d,
    ao_hbm,
    gated_hbm,
    scale_hbm,
    xv,
    zv,
    qv,
    kbuf,
    vbuf,
    k_pass,
    bv,
    cv,
    x_end,
    x_ends,
    rim_x,
    rim_b,
    rim_c,
    xs,
    g1,
    gate,
    e_own,
    e_sib,
    e_chip,
    e_n1,
    e_n2,
    e_pass,
    e_pair,
    chip_decay,
    in_own,
    in_sib,
    t_own,
    t_sib,
    t_chip,
    t_n1,
    sq_own,
    sq_in,
    expand,
    expand_in,
    spread_in,
    shift,
    mix,
    bt,
    cj,
    far_own,
    hot,
    tri_bias,
    ao,
    gated_out,
    scale_out,
    sumsq,
    send,
    recv,
    local,
):
    p = lax.axis_index("ctx")
    t = lax.axis_index("tp")
    core = lax.rem(p, 2)
    sib = p + 1 - 2 * core
    channels = x_hbm.shape[1]
    groups = bv.shape[1] // STATE
    tiles = channels // WIDE
    per_group = tiles // groups
    chip = p // 2
    x_at, z_at = chip // Z_CHIPS, lax.rem(chip, Z_CHIPS)
    x_chips = n_ctx // (2 * Z_CHIPS)

    def chip_device(x, z):
        return (lax.rem(x, x_chips) * Z_CHIPS + lax.rem(z, Z_CHIPS)) * 2 + core

    wraps = ((z_at == 1) | (z_at == 2)).astype(jnp.int32)
    pass_to = chip_device(x_at + wraps, z_at + Z_CHIPS - 1)
    lower = chip_device(x_at, z_at + Z_CHIPS - 1)
    upper = chip_device(x_at, z_at + 1)
    upper_wraps = ((z_at == 0) | (z_at == 1)).astype(jnp.int32)
    pass_from = chip_device(x_at + x_chips - upper_wraps, z_at + 1)

    def at(offset):
        return lax.rem(p + offset + n_ctx, n_ctx)

    def remote(src, dst, slot, to, tp=None):
        return pltpu.make_async_remote_copy(
            src_ref=src,
            dst_ref=dst,
            send_sem=send.at[slot],
            recv_sem=recv.at[slot],
            device_id=(to, t if tp is None else tp),
            device_id_type=MESH,
        )

    last_rows = pl.ds(TOK - 16, 16)
    loads = {
        L_R: pltpu.make_async_copy(x_hbm.at[last_rows], x_end, local.at[L_R]),
        L_B: pltpu.make_async_copy(b_hbm, bv, local.at[L_B]),
        L_C: pltpu.make_async_copy(c_hbm, cv, local.at[L_C]),
        L_X: pltpu.make_async_copy(x_hbm, xv, local.at[L_X]),
        L_Z: pltpu.make_async_copy(z_hbm, zv, local.at[L_Z]),
        L_K: pltpu.make_async_copy(k_hbm, kbuf.at[0], local.at[L_K]),
        L_V: pltpu.make_async_copy(v_hbm, vbuf.at[0], local.at[L_V]),
        L_Q: pltpu.make_async_copy(q_hbm, qv, local.at[L_Q]),
    }

    barrier = pltpu.get_barrier_semaphore()
    for source in (sib, at(-1), at(-2), upper, pass_from):
        pl.semaphore_signal(barrier, inc=1, device_id=(source, t), device_id_type=MESH)
    for step in range(1, n_tp):
        pl.semaphore_signal(
            barrier, inc=1, device_id=(p, lax.rem(t + n_tp - step, n_tp)), device_id_type=MESH
        )
    for slot in (L_R, L_B, L_C, L_X, L_Z, L_K, L_V, L_Q):
        loads[slot].start()
    pl.semaphore_wait(barrier, 5 + n_tp - 1)

    rims = [
        remote(b_hbm.at[last_rows], rim_b, RIM_B, at(1)),
        remote(c_hbm.at[last_rows], rim_c, RIM_C, at(1)),
        remote(x_ends, rim_x, RIM_X, at(1)),
    ]
    k_down = remote(k_hbm, k_pass, KZ, lower)
    for copy in (rims[0], rims[1], k_down):
        copy.start()
    loads[L_R].wait()
    eighth = lax.broadcasted_iota(jnp.int32, (8, WIDE), 0)
    for block in range(tiles // 4):
        ends = [
            x_end[:, (4 * block + i) * WIDE : (4 * block + i + 1) * WIDE].astype(F32)[8:]
            for i in range(4)
        ]
        pairs = [
            jnp.where(eighth < 4, pltpu.roll(ends[i], 4, 0), ends[i + 1]) for i in (0, 2)
        ]
        x_ends[block] = jnp.concatenate(pairs, axis=0).astype(BF16)
    rims[2].start()
    near = [
        remote(v_hbm, vbuf.at[1], V1, at(2)),
        remote(k_hbm, kbuf.at[1], K1, at(2)),
    ]
    far = [
        remote(vbuf.at[1], vbuf.at[3], V2, at(2)),
        remote(k_pass, kbuf.at[3], K2, pass_to),
    ]
    for copy in near:
        copy.start()
    own_to_sib = [
        remote(k_hbm, kbuf.at[4], KX, sib),
        remote(v_hbm, vbuf.at[4], VX, sib),
    ]

    @pl.when(core == 0)
    def _():
        for copy in own_to_sib:
            copy.start()

    def id_row(row):
        return ids[pl.ds(row, 1), :].astype(F32)

    def id_column(row):
        return jnp.broadcast_to(id_row(row), (128, 128)).T

    def id_columns(device):
        return jnp.concatenate([id_column(2 * device), id_column(2 * device + 1)], axis=0)

    own_cols = id_columns(p)
    own_row = jnp.concatenate([id_row(2 * p), id_row(2 * p + 1)], axis=1)
    last_id = own_row[:, TOK - 1 : TOK]
    before_row = lax.rem(2 * p - 1 + 2 * n_ctx, 2 * n_ctx)
    first_device = p == 0
    before_cols = jnp.where(first_device, -1.0, id_column(before_row))
    before_id = jnp.where(first_device, -1.0, id_row(before_row))[:, 127:128]
    lanes = lax.broadcasted_iota(jnp.int32, (TOK, 128), 1).astype(F32)
    row_at = lax.broadcasted_iota(jnp.int32, (TOK, TOK), 0)
    col_at = lax.broadcasted_iota(jnp.int32, (TOK, TOK), 1)
    same = repeat_lanes(own_cols, 2) == own_row
    causal = col_at <= row_at
    allowed = same & causal
    for back in range(1, 4):
        shift[pl.ds((back - 1) * TOK, TOK), :] = jnp.where(
            same & (row_at - col_at == back), 1.0, 0.0
        ).astype(BF16)
    tops = lax.broadcasted_iota(jnp.int32, (8, 128), 0)
    rim_keep = [
        jnp.where(
            (tops < back) & (own_cols[:8] == pltpu.roll(before_cols[120:], back, 0)), 1.0, 0.0
        )
        for back in range(1, 4)
    ]

    raw = dt_raw[...].astype(F32)
    raw = jnp.concatenate([raw, raw], axis=0).T + repeat_lanes(dt_bias[...], 2)
    steps = jnp.maximum(raw, 0.0) + jnp.log(1.0 + jnp.exp(-jnp.abs(raw)))
    log_decay = -steps * repeat_lanes(rates[...], 2)
    upto = jnp.where(causal, 1.0, 0.0).astype(BF16)
    part = log_decay.astype(BF16)
    rest = log_decay - part.astype(F32)
    part2 = rest.astype(BF16)
    part3 = (rest - part2.astype(F32)).astype(BF16)
    cum = dot(upto, part) + (dot(upto, part2) + dot(upto, part3))
    middle = cum[TOK // 2 - 1 : TOK // 2]
    end = cum[TOK - 1 : TOK]
    expand[pl.ds(0, TOK), :] = split2(jnp.exp(middle - cum) * steps)
    expand[pl.ds(TOK, TOK), :] = split2(jnp.exp(cum - middle))
    continues = before_id == last_id
    through = jnp.where(continues, jnp.exp(end), 0.0)
    t_own[...] = jnp.broadcast_to(through, (8, 128))
    t_send = remote(t_own, t_sib, T_SIB, sib)
    t_send.start()

    def spread_matrix(tile):
        head = lax.broadcasted_iota(jnp.int32, (128, WIDE), 0) & 63
        place = (lax.broadcasted_iota(jnp.int32, (128, WIDE), 1) >> 6) + tile * (WIDE // 64)
        return jnp.where(head == place, 1.0, 0.0).astype(BF16)

    def conv(source, rim8, weights, width):
        moved = dot(shift[...], source)
        taps = weights.astype(F32)
        total = taps[3:4] * source.astype(F32)
        edge = jnp.zeros((8, width), F32)
        for back in range(1, 4):
            tap = taps[3 - back : 4 - back]
            total = total + tap * moved[(back - 1) * TOK : back * TOK]
            keep = repeat_lanes(rim_keep[back - 1], width // 128)
            edge = edge + tap * (keep * pltpu.roll(rim8, back, 0))
        total = jnp.concatenate([total[:8] + edge, total[8:]], axis=0)
        return silu(total).astype(BF16)

    loads[L_B].wait()
    rims[0].wait()
    b_conv = conv(bv[...], rim_b[...].astype(F32)[8:], conv_b[...], bv.shape[1])
    for group in range(groups):
        b_group = b_conv[:, group * STATE : (group + 1) * STATE]
        ending = jnp.where(own_cols == last_id, b_group.astype(F32), 0.0)
        bt[group] = ending.T.astype(BF16)

    t_send.wait()
    t_chip[...] = t_own[...] * t_sib[...]
    t_next = remote(t_chip, t_n1, T_C, at(2))
    t_next.start()
    is_low = core == 0
    rows = lax.broadcasted_iota(jnp.int32, (16, 128), 0)
    vectors = jnp.where(rows == 0, jnp.exp(end - middle), 0.0)
    vectors = jnp.where(rows == 1, repeat_lanes(skip_d[...], 2), vectors)
    vectors = jnp.where(rows == 2, jnp.where(is_low, t_sib[0:1], 1.0), vectors)
    vectors = jnp.where(rows == 3, jnp.where(is_low, 1.0, t_own[0:1]), vectors)
    vectors = jnp.where(rows == 4, t_chip[0:1], vectors)
    expand[pl.ds(2 * TOK, 16), :] = split2(vectors)

    loads[L_X].wait()
    rims[2].wait()

    def end_state(first, chunk):
        tile = first + chunk
        here = pl.ds(pl.multiple_of(tile * WIDE, WIDE), WIDE)
        pair = rim_x[first // 4].astype(F32)[8 * (chunk // 2) : 8 * (chunk // 2) + 8]
        rim8 = pltpu.roll(pair, 4, 0) if chunk % 2 == 0 else pair
        x_conv = conv(xv[:, here], rim8, conv_x[:, here], WIDE)
        xv[:, here] = x_conv
        spread = spread_matrix(tile)
        factors = dot(expand[pl.ds(0, TOK), :], spread)
        vectors = dot(expand[pl.ds(2 * TOK, 16), :], spread)
        x_scaled = (x_conv.astype(F32) * factors).astype(BF16)
        xs[:, here] = x_scaled
        state = dot(bt[tile // per_group], x_scaled) * vectors[0:1]
        e_own[tile] = state.astype(BF16)
        return state, vectors

    mine, others = core * CHUNKS, (1 - core) * CHUNKS

    k_down.wait()
    far[1].start()
    halves = [
        remote(e_own.at[others + i], e_sib.at[others + i], E_A + i, sib) for i in range(CHUNKS)
    ]
    odd = lax.rem(z_at, 2) == 1
    firsts = [remote(e_chip.at[i], e_n1.at[i], E1 + i, at(2)) for i in range(PIECES)]
    pairs = [remote(e_pair.at[i], e_n1.at[i], E1 + i, at(2)) for i in range(PIECES)]
    downs = [remote(e_chip.at[i], e_pass.at[i], EZ + i, lower) for i in range(PIECES)]
    passes = [remote(e_pass.at[i], e_n2.at[i], E2 + i, pass_to) for i in range(PIECES)]

    def pass_on(*pieces):
        @pl.when(odd)
        def _():
            for i in pieces:
                chunk, lane = divmod(i * PIECE, WIDE)
                firsts[i].wait_recv()
                e_pair[i] = (
                    e_chip[i].astype(F32)
                    + chip_decay[chunk, 4:5, lane : lane + PIECE] * e_n1[i].astype(F32)
                ).astype(BF16)
                pairs[i].start()

        @pl.when(jnp.logical_not(odd))
        def _():
            for i in pieces:
                downs[i].wait_recv()
                passes[i].start()

    for step in range(CHUNKS + 1):
        if step < CHUNKS:
            end_state(others, step)
            halves[step].start()
        if step == 0:
            near[0].wait()
            far[0].start()
            continue
        chunk = step - 1
        state, vectors = end_state(mine, chunk)
        chip_decay[chunk] = vectors[:8]
        halves[chunk].wait()
        chip_end = (
            vectors[2:3] * state + vectors[3:4] * e_sib[mine + chunk].astype(F32)
        ).astype(BF16)
        for i in range(WIDE // PIECE):
            piece = chunk * (WIDE // PIECE) + i
            e_chip[piece] = chip_end[:, i * PIECE : (i + 1) * PIECE]

            @pl.when(odd)
            def _():
                downs[piece].start()

            @pl.when(jnp.logical_not(odd))
            def _():
                firsts[piece].start()

    half_b = remote(e_own.at[pl.ds(mine, CHUNKS)], e_sib.at[pl.ds(mine, CHUNKS)], E_B, sib)
    half_b.start()
    near[1].wait()
    sib_near = [
        remote(kbuf.at[1], kbuf.at[2], K1S, sib),
        remote(vbuf.at[1], vbuf.at[2], V1S, sib),
    ]
    for copy in sib_near:
        copy.start()

    loads[L_C].wait()
    rims[1].wait()
    c_conv = conv(cv[...], rim_c[...].astype(F32)[8:], conv_c[...], cv.shape[1])
    for group in range(groups):
        b_group = b_conv[:, group * STATE : (group + 1) * STATE]
        c_group = c_conv[:, group * STATE : (group + 1) * STATE]
        mix[group] = jnp.where(allowed, dot_nt(c_group, b_group), 0.0).astype(BF16)
        cj[group] = jnp.where(own_cols == before_id, c_group.astype(F32), 0.0).astype(BF16)

    far_own[...] = jnp.where(own_cols == lanes, 0.0, -FAR).astype(BF16)
    block_devices = (p, p - 2, p - 1 - 2 * core, p - 4, p - 3 + 2 * core)
    for slot, device in enumerate(block_devices):
        columns = id_columns(lax.rem(device + n_ctx, n_ctx)) if slot else own_cols
        hot[slot] = jnp.where(columns == lanes, 1.0, 0.0).astype(BF16)
    tri_bias[...] = jnp.where(causal, 0.0, -FAR)

    loads[L_Z].wait()

    def gate_tile(tile, carry):
        here = pl.ds(pl.multiple_of(tile * WIDE, WIDE), WIDE)
        spread = spread_matrix(tile)
        leaving = dot(expand[pl.ds(TOK, TOK), :], spread)
        vectors = dot(expand[pl.ds(2 * TOK, 16), :], spread)
        open_gate = silu(zv[:, here].astype(F32))
        full = leaving * dot(mix[tile // per_group], xs[:, here]) + vectors[1:2] * xv[
            :, here
        ].astype(F32)
        g1[:, here] = full * open_gate
        gate[:, here] = leaving * open_gate
        return carry

    lax.fori_loop(0, tiles, gate_tile, 0, unroll=2)
    pass_on(0, 1)

    for copy in far:
        copy.wait()
    far_to_sib = [
        remote(kbuf.at[3], kbuf.at[4], KX, sib),
        remote(vbuf.at[3], vbuf.at[4], VX, sib),
    ]

    @pl.when(core == 1)
    def _():
        for copy in far_to_sib:
            copy.start()
        for copy in far_to_sib:
            copy.wait_send()

    @pl.when(core == 0)
    def _():
        for copy in own_to_sib:
            copy.wait_send()

    for copy in far_to_sib:
        copy.wait_recv()
    for copy in sib_near:
        copy.wait()
    for slot in (L_K, L_V, L_Q):
        loads[slot].wait()

    pass_on(2, 3)

    factor = HEAD_DIM**-0.5 * LOG2E
    query_heads = q_hbm.shape[1] // HEAD_DIM
    per_kv = query_heads // (k_hbm.shape[1] // HEAD_DIM)

    def places(head):
        here = pl.ds(pl.multiple_of(head * HEAD_DIM, HEAD_DIM), HEAD_DIM)
        kv = pl.ds(pl.multiple_of((head // per_kv) * HEAD_DIM, HEAD_DIM), HEAD_DIM)
        return here, kv

    def score(head):
        here, kv = places(head)
        query = jnp.concatenate([qv[:, here], far_own[...]], axis=1)
        scores = []
        for slot in range(5):
            key = jnp.concatenate([kbuf[slot, :, kv], hot[slot]], axis=1)
            scores.append(dot_nt(query, key))
        scores[0] = scores[0] + tri_bias[...]
        return scores

    def attend(head, scores):
        here, kv = places(head)
        top = functools.reduce(jnp.maximum, scores)
        top = jnp.max(top, axis=1, keepdims=True) * factor
        ones = jnp.ones((TOK, HEAD_DIM), BF16)
        summed = jnp.zeros((TOK, 2 * HEAD_DIM), F32)
        for slot in range(5):
            weights = jnp.exp2(scores[slot] * factor - top).astype(BF16)
            value = jnp.concatenate([vbuf[slot, :, kv], ones], axis=1)
            summed = summed + dot(weights, value)
        ao[:, here] = (summed[:, :HEAD_DIM] / summed[:, HEAD_DIM:]).astype(BF16)

    per_part = query_heads // CHUNKS

    t_next.wait()
    half_b.wait()
    vectors = jnp.where(rows == 0, jnp.where(is_low, 0.0, jnp.exp(middle)), 0.0)
    vectors = jnp.where(rows == 1, jnp.where(is_low, 1.0, t_sib[0:1]) * jnp.exp(middle), vectors)
    vectors = jnp.where(rows == 2, t_n1[0:1], vectors)
    expand_in[...] = split2(vectors)

    def spread_tile(tile, carry):
        spread_in[tile] = dot(expand_in[...], spread_matrix(tile))
        return carry

    lax.fori_loop(0, tiles, spread_tile, 0)
    sumsq[...] = jnp.zeros_like(sumsq)

    def out_copy(tile, here):
        return pltpu.make_async_copy(
            gated_out.at[:, here], gated_hbm.at[:, here], local.at[L_GATED + tile]
        )

    def join_tile(tile, incoming):
        here = pl.ds(pl.multiple_of(tile * WIDE, WIDE), WIDE)
        vectors = spread_in[tile]
        state = vectors[0:1] * e_sib[tile].astype(F32) + vectors[1:2] * incoming
        gated = g1[:, here] + gate[:, here] * dot(cj[tile // per_group], state.astype(BF16))
        gated_out[:, here] = gated.astype(BF16)
        out_copy(tile, here).start()
        squares = gated * gated
        total = sumsq[...]
        for lane in range(WIDE // 128):
            total = total + squares[:, lane * 128 : (lane + 1) * 128]
        sumsq[...] = total

    swaps = [remote(in_own.at[i], in_sib.at[i], IN + i, sib) for i in range(CHUNKS)]
    sq_sends = [
        remote(sq_own, sq_in.at[step - 1], SQ + step - 1, p, lax.rem(t + step, n_tp))
        for step in range(1, n_tp)
    ]

    def join_all():
        for chunk in range(CHUNKS):
            tile = mine + chunk
            pieces = range(chunk * (WIDE // PIECE), (chunk + 1) * (WIDE // PIECE))

            @pl.when(odd)
            def _():
                for i in pieces:
                    passes[i].wait_recv()
                near_end = jnp.concatenate([e_n1[i] for i in pieces], axis=1).astype(F32)
                far_end = jnp.concatenate([e_n2[i] for i in pieces], axis=1).astype(F32)
                in_own[chunk] = (near_end + spread_in[tile][2:3] * far_end).astype(BF16)

            @pl.when(jnp.logical_not(odd))
            def _():
                for i in pieces:
                    firsts[i].wait_recv()
                in_own[chunk] = jnp.concatenate([e_n1[i] for i in pieces], axis=1)

            swaps[chunk].start()
            join_tile(tile, in_own[chunk].astype(F32))
        for chunk in range(CHUNKS):
            swaps[chunk].wait()
            join_tile(others + chunk, in_sib[chunk].astype(F32))

        own_sums = jnp.concatenate(
            [
                jnp.sum(sumsq[pl.ds(0, 128), :].T, axis=0, keepdims=True),
                jnp.sum(sumsq[pl.ds(128, 128), :].T, axis=0, keepdims=True),
            ],
            axis=1,
        )
        sq_own[...] = jnp.broadcast_to(own_sums, (8, TOK))
        for copy in sq_sends:
            copy.start()

    def attend_part(part, carry):
        first = part * per_part
        following = score(first)
        for i in range(per_part):
            scores = following
            if i + 1 < per_part:
                following = score(first + i + 1)
            attend(first + i, scores)

        @pl.when(part == 0)
        def _():
            pass_on(4, 5)

        @pl.when(part == 1)
        def _():
            pass_on(6, 7)

        @pl.when(part == CHUNKS - 2)
        def _():
            join_all()

        return carry

    lax.fori_loop(0, CHUNKS, attend_part, 0)
    ao_out = pltpu.make_async_copy(ao, ao_hbm, local.at[L_AO])
    ao_out.start()
    for copy in sq_sends:
        copy.wait()

    @pl.when(odd)
    def _():
        for i in range(PIECES):
            downs[i].wait_send()
            pairs[i].wait_send()

    @pl.when(jnp.logical_not(odd))
    def _():
        for i in range(PIECES):
            firsts[i].wait_send()
            passes[i].wait_send()

    total = sq_own[...]
    for step in range(1, n_tp):
        total = total + sq_in[step - 1]
    scale = lax.rsqrt(total[0:1] / INNER + EPSILON)
    scale_cols = jnp.concatenate(
        [
            jnp.broadcast_to(scale[:, :128], (128, 128)).T,
            jnp.broadcast_to(scale[:, 128:], (128, 128)).T,
        ],
        axis=0,
    )
    scale_out[...] = scale_cols
    scale_copy = pltpu.make_async_copy(scale_out, scale_hbm, local.at[L_SCALE])
    scale_copy.start()
    ao_out.wait()
    for tile in range(tiles):
        out_copy(tile, pl.ds(tile * WIDE, WIDE)).wait()
    scale_copy.wait()


def finish(ao_hbm, gated_hbm, scale_hbm, gain_hbm, ao_out, mo_out, ao, gated, scale, gain, mo, sems):
    parts = PARTS
    rows = TOK // parts
    scale_in = pltpu.make_async_copy(scale_hbm, scale, sems.at[0])
    gain_in = pltpu.make_async_copy(gain_hbm, gain, sems.at[1])
    ao_in = pltpu.make_async_copy(ao_hbm, ao, sems.at[2])
    ao_back = pltpu.make_async_copy(ao, ao_out, sems.at[3])

    def part(i):
        return pl.ds(i * rows, rows)

    ins = [
        pltpu.make_async_copy(gated_hbm.at[part(i)], gated.at[part(i)], sems.at[4 + i])
        for i in range(parts)
    ]
    outs = [
        pltpu.make_async_copy(mo.at[part(i)], mo_out.at[part(i)], sems.at[4 + parts + i])
        for i in range(parts)
    ]
    for copy in [scale_in, gain_in, ins[0], ao_in] + ins[1:]:
        copy.start()
    scale_in.wait()
    gain_in.wait()
    for i in range(parts):
        ins[i].wait()
        wide = repeat_lanes(scale[part(i), :], gated.shape[1] // 128)
        mo[part(i), :] = (gated[part(i), :].astype(F32) * wide * gain[...]).astype(BF16)
        outs[i].start()
        if i == 0:
            ao_in.wait()
            ao_back.start()
    ao_back.wait()
    for copy in outs:
        copy.wait()


def per_device(q, k, v, ids, x, b, c, z, dt_raw, conv_x, conv_b, conv_c, dt_bias, rates, skip_d, gain):
    n_ctx, n_tp = lax.axis_size("ctx"), lax.axis_size("tp")
    channels = x.shape[1]
    tiles = channels // WIDE
    groups = b.shape[1] // STATE
    hbm = pl.BlockSpec(memory_space=pl.ANY)
    vmem = pl.BlockSpec(memory_space=pltpu.VMEM)
    specs = [hbm, hbm, hbm, vmem, hbm, hbm, hbm, hbm] + [vmem] * 7
    scratch = [
        pltpu.VMEM(x.shape, BF16),
        pltpu.VMEM(z.shape, BF16),
        pltpu.VMEM(q.shape, BF16),
        pltpu.VMEM((5,) + k.shape, BF16),
        pltpu.VMEM((5,) + v.shape, BF16),
        pltpu.VMEM(k.shape, BF16),
        pltpu.VMEM(b.shape, BF16),
        pltpu.VMEM(c.shape, BF16),
        pltpu.VMEM((16, channels), BF16),
        pltpu.VMEM((tiles // 4, 16, WIDE), BF16),
        pltpu.VMEM((tiles // 4, 16, WIDE), BF16),
        pltpu.VMEM((16, b.shape[1]), BF16),
        pltpu.VMEM((16, c.shape[1]), BF16),
        pltpu.VMEM(x.shape, BF16),
        pltpu.VMEM(x.shape, F32),
        pltpu.VMEM(x.shape, F32),
        pltpu.VMEM((tiles, STATE, WIDE), BF16),
        pltpu.VMEM((tiles, STATE, WIDE), BF16),
        pltpu.VMEM((PIECES, STATE, PIECE), BF16),
        pltpu.VMEM((PIECES, STATE, PIECE), BF16),
        pltpu.VMEM((PIECES, STATE, PIECE), BF16),
        pltpu.VMEM((PIECES, STATE, PIECE), BF16),
        pltpu.VMEM((PIECES, STATE, PIECE), BF16),
        pltpu.VMEM((CHUNKS, 8, WIDE), F32),
        pltpu.VMEM((CHUNKS, STATE, WIDE), BF16),
        pltpu.VMEM((CHUNKS, STATE, WIDE), BF16),
        pltpu.VMEM((8, 128), F32),
        pltpu.VMEM((8, 128), F32),
        pltpu.VMEM((8, 128), F32),
        pltpu.VMEM((8, 128), F32),
        pltpu.VMEM((8, TOK), F32),
        pltpu.VMEM((n_tp - 1, 8, TOK), F32),
        pltpu.VMEM((2 * TOK + 16, 128), BF16),
        pltpu.VMEM((16, 128), BF16),
        pltpu.VMEM((tiles, 16, WIDE), F32),
        pltpu.VMEM((3 * TOK, TOK), BF16),
        pltpu.VMEM((groups, TOK, TOK), BF16),
        pltpu.VMEM((groups, STATE, TOK), BF16),
        pltpu.VMEM((groups, TOK, STATE), BF16),
        pltpu.VMEM((TOK, 128), BF16),
        pltpu.VMEM((5, TOK, 128), BF16),
        pltpu.VMEM((TOK, TOK), F32),
        pltpu.VMEM(q.shape, BF16),
        pltpu.VMEM(x.shape, BF16),
        pltpu.VMEM((TOK, 128), F32),
        pltpu.VMEM((TOK, 128), F32),
        pltpu.SemaphoreType.DMA((COPIES,)),
        pltpu.SemaphoreType.DMA((COPIES,)),
        pltpu.SemaphoreType.DMA((L_GATED + tiles,)),
    ]
    ao, gated, scale = pl.pallas_call(
        functools.partial(kernel, n_ctx, n_tp),
        out_shape=(
            jax.ShapeDtypeStruct(q.shape, BF16),
            jax.ShapeDtypeStruct(x.shape, BF16),
            jax.ShapeDtypeStruct((TOK, 128), F32),
        ),
        in_specs=specs,
        out_specs=(hbm, hbm, hbm),
        scratch_shapes=scratch,
        compiler_params=pltpu.CompilerParams(
            collective_id=1, has_side_effects=True, vmem_limit_bytes=56 * 2**20
        ),
        name="packed_mix",
    )(
        q,
        k,
        v,
        ids.reshape(-1, 128),
        x,
        b,
        c,
        z,
        dt_raw.T,
        conv_x,
        conv_b,
        conv_c,
        dt_bias[None],
        rates[None],
        skip_d[None],
    )
    return pl.pallas_call(
        finish,
        out_shape=(
            jax.ShapeDtypeStruct(q.shape, BF16),
            jax.ShapeDtypeStruct(x.shape, BF16),
        ),
        in_specs=[hbm] * 4,
        out_specs=(hbm, hbm),
        scratch_shapes=[
            pltpu.VMEM(q.shape, BF16),
            pltpu.VMEM(x.shape, BF16),
            pltpu.VMEM((TOK, 128), F32),
            pltpu.VMEM((1, channels), F32),
            pltpu.VMEM(x.shape, BF16),
            pltpu.SemaphoreType.DMA((4 + 2 * PARTS,)),
        ],
        compiler_params=pltpu.CompilerParams(vmem_limit_bytes=60 * 2**20),
        name="scale_rows",
    )(ao, gated, scale, gain[None])


def solution(mesh):
    both = P("ctx", "tp")
    placed = (both, both, both, P(), both, both, both, both, both)
    placed += (P(None, "tp"),) * 3 + (P("tp"),) * 4
    return jax.shard_map(
        per_device, mesh=mesh, in_specs=placed, out_specs=(both, both), check_vma=False
    )
```
